32 devices in a mesh: row: 4 (over z), col: 8 (over y, x, core).
Axes of the slice: x: 2, y: 2, z: 4, core: 2. Of those that a mesh axis runs over, the one named last changes fastest.
Arguments:
- atom_single: bfloat16 [8192, 128], P(('row', 'col')), may hold values from -6 to 6
- atom_token: int32 [8192], P(('row', 'col')), may hold values from 0 to 1023, as said below
- atom_cot: bfloat16 [8192, 128], P(('row', 'col')), may hold values from -6 to 6
- token_cond: bfloat16 [1024, 768], P('row'), may hold values from -6 to 6
- pair: bfloat16 [1024, 1024, 128], P('row', 'col'), may hold values from -12 to 12
- w_pool: bfloat16 [128, 768], replicated, may hold values from -0.5 to 0.5
- w_qkv: bfloat16 [3, 768, 768], P(None, None, 'col'), may hold values from -0.21875 to 0.21875
- w_bias: bfloat16 [128, 16], replicated, may hold values from -0.8 to 0.8
- w_out: bfloat16 [768, 768], P('col'), may hold values from -0.21875 to 0.21875
- w_dec: bfloat16 [768, 128], replicated, may hold values from -0.21875 to 0.21875
Outputs:
- atom_out: bfloat16 [8192, 128], P(('row', 'col'))
- grad_atom: float32 [8192, 128], P(('row', 'col'))
- grad_bias: float32 [128, 16], replicated
The draws below stay inside these ranges and needn't reach their ends.
Inputs may be any that keep to these rules, and one draw needn't show every extreme that they name: `atom_token`: every token has 1 to 24 atoms and some token exactly 24; the atoms stand in no particular order.
All inputs are finite; a program needn't handle non-finite values.
Results may differ from the reference program's by a relative error of at most 0.014.
The reference program's roundings to bfloat16 on the way count: a program that leaves them out, or rounds other values in their place, can miss the bound.
Values may be sent and summed in bfloat16 or wider, within the bound.
A program may use at most 64 MiB of HBM per device.

```python
import math
import jax
import jax.numpy as jnp
from jax import lax

D = 768
H = 16
CA = 128
CP = 128
HD = 48
NTOK = 1024
NATOM = 8192


def bias_base(key):
    return jnp.clip(0.2 * jax.random.normal(key, (CP, H), jnp.float32), -0.8, 0.8)


def draw_w_bias(key, part):
    return bias_base(key).astype(jnp.bfloat16)


def draw_atom_token(key, part):
    key = jax.random.fold_in(key, 11)
    order = jax.random.permutation(jax.random.fold_in(key, 1), NTOK)
    remaining = NTOK - 4
    moves = jax.random.randint(jax.random.fold_in(key, 2), (remaining // 2,), 0, 8).astype(jnp.int32)
    paired = jnp.stack([8 - moves, 8 + moves], axis=1).reshape(remaining)
    ranked = jnp.concatenate([jnp.array([24, 3, 3, 2], jnp.int32), paired])
    sizes = jnp.zeros((NTOK,), jnp.int32).at[order].set(ranked)
    listed = jnp.repeat(jnp.arange(NTOK, dtype=jnp.int32), sizes, total_repeat_length=NATOM)
    return jax.random.permutation(jax.random.fold_in(key, 3), listed).astype(jnp.int32)


def draw_pair(key, part):
    key = jax.random.fold_in(key, 7)
    values = jnp.clip(jax.random.normal(key, (NTOK, NTOK, CP), jnp.float32), -12.0, 12.0)
    return values.astype(jnp.bfloat16)


def block_levels(rng, extent, shards, smallest, top_value):
    def one(axis_at, blocks):
        steps = jax.random.uniform(jax.random.fold_in(jax.random.fold_in(rng, 6), axis_at), (blocks,), jnp.float32, smallest / len(shards), top_value / len(shards))
        return jnp.repeat(jnp.exp(steps), extent[axis_at] // blocks).reshape((-1,) + (1,) * (len(extent) - axis_at - 1))

    loudness = one(*shards[0])
    for cut in shards[1:]:
        loudness = loudness * one(*cut)
    return loudness


def gaussian(stream_key, shape, spread, most, split=(), kind=jnp.bfloat16):
    drawn = jax.random.normal(stream_key, shape, jnp.float32) * spread
    if len(split) > 0:
        drawn = block_levels(stream_key, shape, split, -0.22, 0.18) * drawn
    return jnp.clip(drawn, min=-most, max=most).astype(kind)


def setup_inputs(seed: int = 0) -> dict:
    splits = jax.random.split(jax.random.key(seed), 11)
    return {
        "atom_single": gaussian(splits[0], (NATOM, CA), 1.0, 6.0, ((0, 32),)),
        "atom_token": draw_atom_token(jax.random.fold_in(splits[10], 71), 0),
        "atom_cot": gaussian(splits[2], (NATOM, CA), 1.0, 6.0, ((0, 32),)),
        "token_cond": gaussian(splits[3], (NTOK, D), 1.0, 6.0, ((0, 4),)),
        "pair": draw_pair(jax.random.fold_in(splits[10], 71), 0),
        "w_pool": gaussian(splits[5], (CA, D), CA ** -0.5, 0.5),
        "w_qkv": gaussian(splits[6], (3, D, D), D ** -0.5, 0.21875, ((2, 8),)),
        "w_bias": draw_w_bias(jax.random.fold_in(splits[10], 71), 0),
        "w_out": gaussian(splits[8], (D, D), D ** -0.5, 0.21875, ((0, 8),)),
        "w_dec": gaussian(splits[9], (D, CA), D ** -0.5, 0.21875),
    }


EPSILON = 1e-05

def layer_norm(single):
    center = single - lax.optimization_barrier(jnp.mean(single, axis=-1, keepdims=True))
    inverse = lax.rsqrt(lax.optimization_barrier(jnp.mean(center * center, axis=-1, keepdims=True)) + EPSILON)
    return (center * inverse, inverse)

def norm_grad(upstream, normal, inverse):
    return inverse * (upstream - lax.optimization_barrier(jnp.mean(upstream, axis=-1, keepdims=True)) - normal * lax.optimization_barrier(jnp.mean(upstream * normal, axis=-1, keepdims=True)))

def split_heads(matrix):
    return jnp.transpose(matrix.reshape(NTOK, H, HD), (1, 0, 2))

def merge_heads(stacked):
    return jnp.transpose(stacked, (1, 0, 2)).reshape(NTOK, D)

def reference(atom_single, atom_token, atom_cot, token_cond, pair, w_pool, w_qkv, w_bias, w_out, w_dec):
    ones_atom = jnp.ones(atom_token.shape, jnp.float32)
    counts = jax.ops.segment_sum(ones_atom, atom_token, num_segments=NTOK)
    sums = jax.ops.segment_sum(atom_single.astype(jnp.float32), atom_token, num_segments=NTOK)
    cot_sums = jax.ops.segment_sum(atom_cot.astype(jnp.float32), atom_token, num_segments=NTOK)
    pooled = (sums / counts[:, None]).astype(jnp.bfloat16)
    cot_pooled = cot_sums.astype(jnp.bfloat16)
    single = token_cond.astype(jnp.float32) + jnp.dot(pooled, w_pool, preferred_element_type=jnp.float32)
    normal, inverse = layer_norm(single)
    normed = normal.astype(jnp.bfloat16)
    queries = jnp.dot(normed, w_qkv[0], preferred_element_type=jnp.float32).astype(jnp.bfloat16)
    keys = jnp.dot(normed, w_qkv[1], preferred_element_type=jnp.float32).astype(jnp.bfloat16)
    values = jnp.dot(normed, w_qkv[2], preferred_element_type=jnp.float32).astype(jnp.bfloat16)
    grad_out = jnp.dot(cot_pooled, w_dec.T, preferred_element_type=jnp.float32)
    grad_update = grad_out.astype(jnp.bfloat16)
    grad_attended = jnp.dot(grad_update, w_out.T, preferred_element_type=jnp.float32).astype(jnp.bfloat16)
    bias = jnp.dot(pair.reshape(NTOK * NTOK, CP), w_bias, preferred_element_type=jnp.float32).astype(jnp.bfloat16)
    bias_heads = jnp.transpose(bias.reshape(NTOK, NTOK, H), (2, 0, 1))
    scale = 1.0 / math.sqrt(HD)

    def per_head(items):
        head_q, head_k, head_v, head_bias, head_grad = items
        logits = jnp.dot(head_q, head_k.T, preferred_element_type=jnp.float32) * scale + head_bias.astype(jnp.float32)
        shifted = jnp.exp(logits - lax.optimization_barrier(jnp.max(logits, axis=-1, keepdims=True)))
        probs = shifted / lax.optimization_barrier(jnp.sum(shifted, axis=-1, keepdims=True))
        probs_low = probs.astype(jnp.bfloat16)
        attended = jnp.dot(probs_low, head_v, preferred_element_type=jnp.float32).astype(jnp.bfloat16)
        grad_probs = jnp.dot(head_grad, head_v.T, preferred_element_type=jnp.float32)
        delta = lax.optimization_barrier(jnp.sum(probs * grad_probs, axis=-1, keepdims=True))
        grad_logits = (probs * (grad_probs - delta)).astype(jnp.bfloat16)
        grad_q = (jnp.dot(grad_logits, head_k, preferred_element_type=jnp.float32) * scale).astype(jnp.bfloat16)
        grad_k = (jnp.dot(grad_logits.T, head_q, preferred_element_type=jnp.float32) * scale).astype(jnp.bfloat16)
        grad_v = jnp.dot(probs_low.T, head_grad, preferred_element_type=jnp.float32).astype(jnp.bfloat16)
        return (attended, grad_logits, grad_q, grad_k, grad_v)
    attended, grad_logits, grad_q, grad_k, grad_v = lax.map(per_head, (split_heads(queries), split_heads(keys), split_heads(values), bias_heads, split_heads(grad_attended)))
    update = jnp.dot(merge_heads(attended), w_out, preferred_element_type=jnp.float32)
    token_out = (single + update).astype(jnp.bfloat16)
    token_back = jnp.dot(token_out, w_dec, preferred_element_type=jnp.float32).astype(jnp.bfloat16)
    atom_out = (atom_single.astype(jnp.float32) + token_back[atom_token].astype(jnp.float32)).astype(jnp.bfloat16)
    logit_rows = jnp.transpose(grad_logits, (1, 2, 0)).reshape(NTOK * NTOK, H)
    grad_bias = jnp.dot(pair.reshape(NTOK * NTOK, CP).T, logit_rows, preferred_element_type=jnp.float32)
    grad_normed = jnp.dot(merge_heads(grad_q), w_qkv[0].T, preferred_element_type=jnp.float32)
    grad_normed = grad_normed + jnp.dot(merge_heads(grad_k), w_qkv[1].T, preferred_element_type=jnp.float32)
    grad_normed = grad_normed + jnp.dot(merge_heads(grad_v), w_qkv[2].T, preferred_element_type=jnp.float32)
    grad_single = (grad_out + norm_grad(grad_normed, normal, inverse)).astype(jnp.bfloat16)
    token_grad = (jnp.dot(grad_single, w_pool.T, preferred_element_type=jnp.float32) / counts[:, None]).astype(jnp.bfloat16)
    grad_atom = atom_cot.astype(jnp.float32) + token_grad[atom_token].astype(jnp.float32)
    return (atom_out, grad_atom, grad_bias)
```

```python
import math

import jax
import jax.numpy as jnp
from jax import lax
from jax.sharding import PartitionSpec as P

HD = 48


EPSILON = 1e-05


def layer_norm(single):
    center = single - jnp.mean(single, axis=-1, keepdims=True)
    inverse = lax.rsqrt(jnp.mean(center * center, axis=-1, keepdims=True) + EPSILON)
    return (center * inverse, inverse)


def norm_grad(upstream, normal, inverse):
    return inverse * (
        upstream
        - jnp.mean(upstream, axis=-1, keepdims=True)
        - normal * jnp.mean(upstream * normal, axis=-1, keepdims=True)
    )


def transposed_dot(left, right):
    return lax.dot_general(
        left, right, (((1,), (1,)), ((), ())), preferred_element_type=jnp.float32
    )


def exchange_blocks(blocks, axis):
    return lax.all_to_all(blocks, axis, split_axis=0, concat_axis=0, tiled=True)


def exchange(rows, axis):
    return exchange_blocks(rows.reshape(lax.axis_size(axis), -1, rows.shape[-1]), axis)


def gather(block, axis):
    return exchange_blocks(
        jnp.broadcast_to(block[None], (lax.axis_size(axis),) + block.shape), axis
    )


def share_order(token, tok_rows, share):
    row, inside = token // tok_rows, token % tok_rows
    return (inside // share * lax.axis_size("row") + row) * share + inside % share


def split_two(values):
    high = lax.reduce_precision(values, exponent_bits=8, mantissa_bits=7)
    return jnp.concatenate([high, values - high], axis=-1).astype(jnp.bfloat16)


def join_two(terms):
    high, low = jnp.split(terms.astype(jnp.float32), 2, axis=-1)
    return high + low


def on_device(
    atom_single, atom_token, atom_cot, token_cond, pair, w_pool, w_qkv, w_bias, w_out, w_dec
):
    tok_rows = token_cond.shape[0]
    total_tokens = tok_rows * lax.axis_size("row")
    width = w_out.shape[0]
    local_heads = width // HD
    atom_width = atom_single.shape[1]
    scale = 1.0 / math.sqrt(HD)
    share = tok_rows // lax.axis_size("col")
    onehot = (
        share_order(atom_token, tok_rows, share)[:, None]
        == jnp.arange(total_tokens, dtype=jnp.int32)[None, :]
    ).astype(jnp.bfloat16)
    stacked = jnp.concatenate([atom_single, atom_cot, jnp.ones_like(atom_cot)], axis=1)
    partial_sums = lax.dot_general(
        onehot, stacked, (((0,), (0,)), ((), ())), preferred_element_type=jnp.float32
    ).astype(jnp.bfloat16)
    col_sums = jnp.sum(exchange(partial_sums, "col").astype(jnp.float32), axis=0)
    share_sums = jnp.sum(exchange(col_sums, "row"), axis=0)
    share_counts = share_sums[:, 2 * atom_width :]
    share_rows = jnp.concatenate(
        [
            share_sums[:, :atom_width] / share_counts,
            share_sums[:, atom_width:],
        ],
        axis=1,
    ).astype(jnp.bfloat16)
    row_pooled = gather(share_rows, "col").reshape(tok_rows, 3 * atom_width)
    pooled = row_pooled[:, :atom_width]
    cot_pooled = row_pooled[:, atom_width : 2 * atom_width]
    single = token_cond.astype(jnp.float32) + jnp.dot(
        pooled, w_pool, preferred_element_type=jnp.float32
    )
    normal, inverse = layer_norm(single)
    normed = normal.astype(jnp.bfloat16)
    projected = jnp.einsum("td,kdf->ktf", normed, w_qkv, preferred_element_type=jnp.float32).astype(
        jnp.bfloat16
    )
    gathered = jnp.swapaxes(gather(projected[1:], "row"), 0, 1)
    queries = projected[0].reshape(tok_rows, local_heads, HD)
    keys_all = gathered[0].reshape(total_tokens, local_heads, HD)
    values_all = gathered[1].reshape(total_tokens, local_heads, HD)
    bias_local = jnp.einsum("ijc,ch->hij", pair, w_bias, preferred_element_type=jnp.float32).astype(
        jnp.bfloat16
    )
    bias_rows = lax.all_to_all(bias_local, "col", split_axis=0, concat_axis=2, tiled=True)
    logits = jnp.einsum(
        "ihd,jhd->hij", queries, keys_all, preferred_element_type=jnp.float32
    ) * scale + bias_rows.astype(jnp.float32)
    shifted = jnp.exp(logits - jnp.max(logits, axis=-1, keepdims=True))
    probs = shifted / jnp.sum(shifted, axis=-1, keepdims=True)
    probs_low = probs.astype(jnp.bfloat16)
    attended = (
        jnp.einsum("hij,jhd->ihd", probs_low, values_all, preferred_element_type=jnp.float32)
        .astype(jnp.bfloat16)
        .reshape(tok_rows, width)
    )
    partial_update = jnp.dot(attended, w_out, preferred_element_type=jnp.float32)
    grad_out = transposed_dot(cot_pooled, w_dec)
    grad_update = grad_out.astype(jnp.bfloat16)
    grad_attended = (
        transposed_dot(grad_update, w_out).astype(jnp.bfloat16).reshape(tok_rows, local_heads, HD)
    )
    grad_probs = jnp.einsum(
        "ihd,jhd->hij", grad_attended, values_all, preferred_element_type=jnp.float32
    )
    delta = jnp.sum(probs * grad_probs, axis=-1, keepdims=True)
    grad_logits = (probs * (grad_probs - delta)).astype(jnp.bfloat16)
    grad_queries = (
        (
            jnp.einsum("hij,jhd->ihd", grad_logits, keys_all, preferred_element_type=jnp.float32)
            * scale
        )
        .astype(jnp.bfloat16)
        .reshape(tok_rows, width)
    )
    key_terms = jnp.stack(
        [
            jnp.einsum("hij,ihd->jhd", grad_logits, queries, preferred_element_type=jnp.float32),
            jnp.einsum(
                "hij,ihd->jhd", probs_low, grad_attended, preferred_element_type=jnp.float32
            ),
        ]
    ).reshape(2, total_tokens, width)
    key_blocks = jnp.swapaxes(
        key_terms.astype(jnp.bfloat16).reshape(2, -1, tok_rows, width), 0, 1
    )
    key_sums = jnp.sum(exchange_blocks(key_blocks, "row").astype(jnp.float32), axis=0)
    grad_keys = (key_sums[0] * scale).astype(jnp.bfloat16)
    grad_values = key_sums[1].astype(jnp.bfloat16)
    grad_proj = jnp.stack([grad_queries, grad_keys, grad_values])
    normed_part = jnp.einsum("ktf,kdf->td", grad_proj, w_qkv, preferred_element_type=jnp.float32)
    width_all = partial_update.shape[1]
    both = jnp.concatenate([partial_update, normed_part], axis=1).astype(jnp.bfloat16)
    bias_back = lax.all_to_all(grad_logits, "col", split_axis=2, concat_axis=0, tiled=True)
    both_sums = jnp.sum(exchange(both, "col").astype(jnp.float32), axis=0)
    weight_part = jnp.einsum("ijc,hij->hc", pair, bias_back, preferred_element_type=jnp.float32)

    def mine(rows):
        return lax.dynamic_slice_in_dim(rows, lax.axis_index("col") * share, share, axis=0)

    token_out = (mine(single) + both_sums[:, :width_all]).astype(jnp.bfloat16)
    token_back = jnp.dot(token_out, w_dec, preferred_element_type=jnp.float32).astype(jnp.bfloat16)
    grad_normed = both_sums[:, width_all:]
    grad_single = (mine(grad_out) + norm_grad(grad_normed, mine(normal), mine(inverse))).astype(
        jnp.bfloat16
    )
    token_grad = (transposed_dot(grad_single, w_pool) / share_counts[:, :atom_width]).astype(
        jnp.bfloat16
    )
    share_back = jnp.concatenate([token_back, token_grad], axis=1)
    first = gather(jnp.concatenate([share_back, split_two(weight_part)], axis=0), "row")
    row_weight = jnp.sum(join_two(first[:, share:]), axis=0)
    second = gather(
        jnp.concatenate(
            [first[:, :share].reshape(-1, 2 * atom_width), split_two(row_weight)], axis=0
        ),
        "col",
    )
    grad_bias = jnp.sum(join_two(second[:, -weight_part.shape[0] :]), axis=0).T
    all_back = second[:, : -weight_part.shape[0]].reshape(total_tokens, 2 * atom_width)
    picked = jnp.dot(onehot, all_back, preferred_element_type=jnp.float32)
    atom_out = (atom_single.astype(jnp.float32) + picked[:, :atom_width]).astype(jnp.bfloat16)
    grad_atom = atom_cot.astype(jnp.float32) + picked[:, atom_width:]
    return (atom_out, grad_atom, grad_bias)


def solution(mesh):
    return jax.shard_map(
        on_device,
        mesh=mesh,
        in_specs=(
            P(("row", "col"), None),
            P(("row", "col")),
            P(("row", "col"), None),
            P("row", None),
            P("row", "col", None),
            P(),
            P(None, None, "col"),
            P(),
            P("col", None),
            P(),
        ),
        out_specs=(P(("row", "col"), None), P(("row", "col"), None), P()),
        check_vma=False,
    )
```

```python
import functools
import math

import jax
import jax.numpy as jnp
from jax import lax
from jax.experimental import pallas as pl
from jax.experimental.pallas import tpu as pltpu
from jax.sharding import PartitionSpec as P

HD = 48


EPSILON = 1e-05


def layer_norm(single):
    center = single - jnp.mean(single, axis=-1, keepdims=True)
    inverse = lax.rsqrt(jnp.mean(center * center, axis=-1, keepdims=True) + EPSILON)
    return (center * inverse, inverse)


def norm_grad(upstream, normal, inverse):
    return inverse * (
        upstream
        - jnp.mean(upstream, axis=-1, keepdims=True)
        - normal * jnp.mean(upstream * normal, axis=-1, keepdims=True)
    )


def transposed_dot(left, right):
    return lax.dot_general(
        left, right, (((1,), (1,)), ((), ())), preferred_element_type=jnp.float32
    )


def exchange_blocks(blocks, axis):
    return lax.all_to_all(blocks, axis, split_axis=0, concat_axis=0, tiled=True)


def gather(block, axis):
    return exchange_blocks(
        jnp.broadcast_to(block[None], (lax.axis_size(axis),) + block.shape), axis
    )


def share_order(token, tok_rows, share):
    row, inside = token // tok_rows, token % tok_rows
    return (inside // share * lax.axis_size("row") + row) * share + inside % share


def push(source, target, send_sems, recv_sems, at, axis, peer):
    copy = pltpu.make_async_remote_copy(
        src_ref=source,
        dst_ref=target,
        send_sem=send_sems.at[at],
        recv_sem=recv_sems.at[at],
        device_id={axis: peer},
        device_id_type=pl.DeviceIdType.MESH,
    )
    copy.start()
    return copy


def peers_of(axis, size):
    me = lax.axis_index(axis)
    return [(step, lax.rem(me + step, size)) for step in range(1, size)]


def greet(sizes):
    barrier = pltpu.get_barrier_semaphore()
    for axis, size in sizes:
        for _, peer in peers_of(axis, size):
            pl.semaphore_signal(
                barrier, inc=1, device_id={axis: peer}, device_id_type=pl.DeviceIdType.MESH
            )
    pl.semaphore_wait(barrier, sum(size - 1 for _, size in sizes))


def pool_kernel(
    rows, cols, sums_ref, out_ref, counts_ref, got_col, col_sum, got_row, send_sems, recv_sems
):
    row, col = lax.axis_index("row"), lax.axis_index("col")
    greet((("row", rows), ("col", cols)))
    width = out_ref.shape[-1] // 3
    copies = [
        push(sums_ref.at[peer], got_col.at[step - 1], send_sems, recv_sems, step - 1, "col", peer)
        for step, peer in peers_of("col", cols)
    ]
    total = sums_ref[col].astype(jnp.float32)
    for at, copy in enumerate(copies):
        copy.wait()
        total = total + got_col[at].astype(jnp.float32)
    col_sum[...] = total.reshape(col_sum.shape)
    base = cols - 1
    copies = [
        push(
            col_sum.at[peer],
            got_row.at[step - 1],
            send_sems,
            recv_sems,
            base + step - 1,
            "row",
            peer,
        )
        for step, peer in peers_of("row", rows)
    ]
    total = col_sum[row]
    for at, copy in enumerate(copies):
        copy.wait()
        total = total + got_row[at]
    counts = total[:, 2 * width :]
    counts_ref[...] = counts
    out_ref[col] = jnp.concatenate(
        [total[:, :width] / counts, total[:, width:]], axis=1
    ).astype(out_ref.dtype)
    base += rows - 1
    copies = [
        push(
            out_ref.at[col], out_ref.at[col], send_sems, recv_sems, base + step - 1, "col", peer
        )
        for step, peer in peers_of("col", cols)
    ]
    for copy in copies:
        copy.wait()


def pool_call(partial_sums, share):
    rows, cols = lax.axis_size("row"), lax.axis_size("col")
    width = partial_sums.shape[-1]
    copies = 2 * (cols - 1) + rows - 1
    return pl.pallas_call(
        functools.partial(pool_kernel, rows, cols),
        out_shape=(
            jax.ShapeDtypeStruct((cols, share, width), jnp.bfloat16),
            jax.ShapeDtypeStruct((share, width // 3), jnp.float32),
        ),
        in_specs=[pl.BlockSpec(memory_space=pltpu.VMEM)],
        out_specs=(pl.BlockSpec(memory_space=pltpu.VMEM),) * 2,
        scratch_shapes=[
            pltpu.VMEM((cols - 1, rows * share, width), jnp.bfloat16),
            pltpu.VMEM((rows, share, width), jnp.float32),
            pltpu.VMEM((rows - 1, share, width), jnp.float32),
            pltpu.SemaphoreType.DMA((copies,)),
            pltpu.SemaphoreType.DMA((copies,)),
        ],
        compiler_params=pltpu.CompilerParams(collective_id=0, has_side_effects=True),
    )(partial_sums.reshape(cols, rows * share, width))


def tail_kernel(
    rows,
    cols,
    both_ref,
    single_ref,
    grad_out_ref,
    normal_ref,
    inverse_ref,
    counts_ref,
    dec_ref,
    pool_ref,
    weight_ref,
    out_ref,
    weight_out_ref,
    got_both,
    held,
    row_weights,
    col_weights,
    send_sems,
    recv_sems,
):
    row, col = lax.axis_index("row"), lax.axis_index("col")
    greet((("row", rows), ("col", cols)))
    width = single_ref.shape[-1]
    copies = [
        push(both_ref.at[peer], got_both.at[step - 1], send_sems, recv_sems, step - 1, "col", peer)
        for step, peer in peers_of("col", cols)
    ]
    base = cols - 1
    row_weights[row] = weight_ref[...]
    weight_copies = [
        push(
            row_weights.at[row],
            row_weights.at[row],
            send_sems,
            recv_sems,
            base + step - 1,
            "row",
            peer,
        )
        for step, peer in peers_of("row", rows)
    ]
    base += rows - 1
    total = both_ref[col].astype(jnp.float32)
    for at, copy in enumerate(copies):
        copy.wait()
        total = total + got_both[at].astype(jnp.float32)
    token_out = (single_ref[...] + total[:, :width]).astype(jnp.bfloat16)
    token_back = jnp.dot(token_out, dec_ref[...], preferred_element_type=jnp.float32)
    grad_single = (
        grad_out_ref[...] + norm_grad(total[:, width:], normal_ref[...], inverse_ref[...])
    ).astype(jnp.bfloat16)
    token_grad = transposed_dot(grad_single, pool_ref[...]) / counts_ref[...]
    held[row] = jnp.concatenate([token_back, token_grad], axis=1).astype(jnp.bfloat16)
    copies = [
        push(held.at[row], held.at[row], send_sems, recv_sems, base + step - 1, "row", peer)
        for step, peer in peers_of("row", rows)
    ]
    base += rows - 1
    for copy in weight_copies:
        copy.wait()
    weight = row_weights[0]
    for at in range(1, rows):
        weight = weight + row_weights[at]
    col_weights[col] = weight
    weight_copies = [
        push(
            col_weights.at[col],
            col_weights.at[col],
            send_sems,
            recv_sems,
            base + step - 1,
            "col",
            peer,
        )
        for step, peer in peers_of("col", cols)
    ]
    base += cols - 1
    for copy in copies:
        copy.wait()
    copies = [
        push(held, out_ref.at[col], send_sems, recv_sems, base + step - 1, "col", peer)
        for step, peer in peers_of("col", cols)
    ]
    out_ref[col] = held[...]
    for copy in weight_copies:
        copy.wait()
    weight = col_weights[0]
    for at in range(1, cols):
        weight = weight + col_weights[at]
    weight_out_ref[...] = weight
    for copy in copies:
        copy.wait()


def tail_call(both, single, grad_out, normal, inverse, counts, w_dec, w_pool, weight):
    rows, cols = lax.axis_size("row"), lax.axis_size("col")
    share, atom_width = counts.shape
    copies = 3 * (cols - 1) + 2 * (rows - 1)
    return pl.pallas_call(
        functools.partial(tail_kernel, rows, cols),
        out_shape=(
            jax.ShapeDtypeStruct((cols, rows, share, 2 * atom_width), jnp.bfloat16),
            jax.ShapeDtypeStruct(weight.shape, jnp.float32),
        ),
        in_specs=[pl.BlockSpec(memory_space=pltpu.VMEM)] * 9,
        out_specs=(pl.BlockSpec(memory_space=pltpu.VMEM),) * 2,
        scratch_shapes=[
            pltpu.VMEM((cols - 1, share, both.shape[-1]), jnp.bfloat16),
            pltpu.VMEM((rows, share, 2 * atom_width), jnp.bfloat16),
            pltpu.VMEM((rows,) + weight.shape, jnp.float32),
            pltpu.VMEM((cols,) + weight.shape, jnp.float32),
            pltpu.SemaphoreType.DMA((copies,)),
            pltpu.SemaphoreType.DMA((copies,)),
        ],
        compiler_params=pltpu.CompilerParams(collective_id=1, has_side_effects=True),
    )(
        both.reshape(cols, share, -1),
        single,
        grad_out,
        normal,
        inverse,
        counts,
        w_dec,
        w_pool,
        weight,
    )


def on_device(
    atom_single, atom_token, atom_cot, token_cond, pair, w_pool, w_qkv, w_bias, w_out, w_dec
):
    tok_rows = token_cond.shape[0]
    total_tokens = tok_rows * lax.axis_size("row")
    width = w_out.shape[0]
    local_heads = width // HD
    atom_width = atom_single.shape[1]
    scale = 1.0 / math.sqrt(HD)
    share = tok_rows // lax.axis_size("col")
    onehot = (
        share_order(atom_token, tok_rows, share)[:, None]
        == jnp.arange(total_tokens, dtype=jnp.int32)[None, :]
    ).astype(jnp.bfloat16)
    stacked = jnp.concatenate([atom_single, atom_cot, jnp.ones_like(atom_cot)], axis=1)
    partial_sums = lax.dot_general(
        onehot, stacked, (((0,), (0,)), ((), ())), preferred_element_type=jnp.float32
    ).astype(jnp.bfloat16)
    row_pooled, share_counts = pool_call(partial_sums, share)
    row_pooled = row_pooled.reshape(tok_rows, 3 * atom_width)
    pooled = row_pooled[:, :atom_width]
    cot_pooled = row_pooled[:, atom_width : 2 * atom_width]
    single = token_cond.astype(jnp.float32) + jnp.dot(
        pooled, w_pool, preferred_element_type=jnp.float32
    )
    normal, inverse = layer_norm(single)
    normed = normal.astype(jnp.bfloat16)
    projected = jnp.einsum("td,kdf->ktf", normed, w_qkv, preferred_element_type=jnp.float32).astype(
        jnp.bfloat16
    )
    gathered = jnp.swapaxes(gather(projected[1:], "row"), 0, 1)
    queries = projected[0].reshape(tok_rows, local_heads, HD)
    keys_all = gathered[0].reshape(total_tokens, local_heads, HD)
    values_all = gathered[1].reshape(total_tokens, local_heads, HD)
    bias_local = jnp.einsum("ijc,ch->hij", pair, w_bias, preferred_element_type=jnp.float32).astype(
        jnp.bfloat16
    )
    bias_rows = lax.all_to_all(bias_local, "col", split_axis=0, concat_axis=2, tiled=True)
    logits = jnp.einsum(
        "ihd,jhd->hij", queries, keys_all, preferred_element_type=jnp.float32
    ) * scale + bias_rows.astype(jnp.float32)
    shifted = jnp.exp(logits - jnp.max(logits, axis=-1, keepdims=True))
    probs = shifted / jnp.sum(shifted, axis=-1, keepdims=True)
    probs_low = probs.astype(jnp.bfloat16)
    attended = (
        jnp.einsum("hij,jhd->ihd", probs_low, values_all, preferred_element_type=jnp.float32)
        .astype(jnp.bfloat16)
        .reshape(tok_rows, width)
    )
    partial_update = jnp.dot(attended, w_out, preferred_element_type=jnp.float32)
    grad_out = transposed_dot(cot_pooled, w_dec)
    grad_update = grad_out.astype(jnp.bfloat16)
    grad_attended = (
        transposed_dot(grad_update, w_out).astype(jnp.bfloat16).reshape(tok_rows, local_heads, HD)
    )
    grad_probs = jnp.einsum(
        "ihd,jhd->hij", grad_attended, values_all, preferred_element_type=jnp.float32
    )
    delta = jnp.sum(probs * grad_probs, axis=-1, keepdims=True)
    grad_logits = (probs * (grad_probs - delta)).astype(jnp.bfloat16)
    grad_queries = (
        (
            jnp.einsum("hij,jhd->ihd", grad_logits, keys_all, preferred_element_type=jnp.float32)
            * scale
        )
        .astype(jnp.bfloat16)
        .reshape(tok_rows, width)
    )
    key_terms = jnp.stack(
        [
            jnp.einsum("hij,ihd->jhd", grad_logits, queries, preferred_element_type=jnp.float32),
            jnp.einsum(
                "hij,ihd->jhd", probs_low, grad_attended, preferred_element_type=jnp.float32
            ),
        ]
    ).reshape(2, total_tokens, width)
    key_blocks = jnp.swapaxes(
        key_terms.astype(jnp.bfloat16).reshape(2, -1, tok_rows, width), 0, 1
    )
    key_sums = jnp.sum(exchange_blocks(key_blocks, "row").astype(jnp.float32), axis=0)
    grad_keys = (key_sums[0] * scale).astype(jnp.bfloat16)
    grad_values = key_sums[1].astype(jnp.bfloat16)
    grad_proj = jnp.stack([grad_queries, grad_keys, grad_values])
    normed_part = jnp.einsum("ktf,kdf->td", grad_proj, w_qkv, preferred_element_type=jnp.float32)
    both = jnp.concatenate([partial_update, normed_part], axis=1).astype(jnp.bfloat16)
    bias_back = lax.all_to_all(grad_logits, "col", split_axis=2, concat_axis=0, tiled=True)
    weight_part = jnp.einsum("ijc,hij->hc", pair, bias_back, preferred_element_type=jnp.float32)

    def mine(rows):
        return lax.dynamic_slice_in_dim(rows, lax.axis_index("col") * share, share, axis=0)

    all_back, grad_bias = tail_call(
        both,
        mine(single),
        mine(grad_out),
        mine(normal),
        mine(inverse),
        share_counts,
        w_dec,
        w_pool,
        weight_part,
    )
    all_back = all_back.reshape(total_tokens, 2 * atom_width)
    grad_bias = grad_bias.T
    picked = jnp.dot(onehot, all_back, preferred_element_type=jnp.float32)
    atom_out = (atom_single.astype(jnp.float32) + picked[:, :atom_width]).astype(jnp.bfloat16)
    grad_atom = atom_cot.astype(jnp.float32) + picked[:, atom_width:]
    return (atom_out, grad_atom, grad_bias)


def solution(mesh):
    return jax.shard_map(
        on_device,
        mesh=mesh,
        in_specs=(
            P(("row", "col"), None),
            P(("row", "col")),
            P(("row", "col"), None),
            P("row", None),
            P("row", "col", None),
            P(),
            P(None, None, "col"),
            P(),
            P("col", None),
            P(),
        ),
        out_specs=(P(("row", "col"), None), P(("row", "col"), None), P()),
        check_vma=False,
    )
```

```python
import functools
import math

import jax
import jax.numpy as jnp
from jax import lax
from jax.experimental import pallas as pl
from jax.experimental.pallas import tpu as pltpu
from jax.sharding import PartitionSpec as P

HD = 48


EPSILON = 1e-05


def layer_norm(single):
    center = single - jnp.mean(single, axis=-1, keepdims=True)
    inverse = lax.rsqrt(jnp.mean(center * center, axis=-1, keepdims=True) + EPSILON)
    return (center * inverse, inverse)


def norm_grad(upstream, normal, inverse):
    return inverse * (
        upstream
        - jnp.mean(upstream, axis=-1, keepdims=True)
        - normal * jnp.mean(upstream * normal, axis=-1, keepdims=True)
    )


def transposed_dot(left, right):
    return lax.dot_general(
        left, right, (((1,), (1,)), ((), ())), preferred_element_type=jnp.float32
    )


def exchange_blocks(blocks, axis):
    return lax.all_to_all(blocks, axis, split_axis=0, concat_axis=0, tiled=True)


def gather(block, axis):
    return exchange_blocks(
        jnp.broadcast_to(block[None], (lax.axis_size(axis),) + block.shape), axis
    )


def share_order(token, tok_rows, share):
    row, inside = token // tok_rows, token % tok_rows
    return (inside // share * lax.axis_size("row") + row) * share + inside % share


def push(source, target, send_sems, recv_sems, at, axis, peer):
    copy = pltpu.make_async_remote_copy(
        src_ref=source,
        dst_ref=target,
        send_sem=send_sems.at[at],
        recv_sem=recv_sems.at[at],
        device_id={axis: peer},
        device_id_type=pl.DeviceIdType.MESH,
    )
    copy.start()
    return copy


def peers_of(axis, size):
    me = lax.axis_index(axis)
    return [(step, lax.rem(me + step, size)) for step in range(1, size)]


def greet(sizes):
    barrier = pltpu.get_barrier_semaphore()
    for axis, size in sizes:
        for _, peer in peers_of(axis, size):
            pl.semaphore_signal(
                barrier, inc=1, device_id={axis: peer}, device_id_type=pl.DeviceIdType.MESH
            )
    pl.semaphore_wait(barrier, sum(size - 1 for _, size in sizes))


def pool_kernel(
    rows,
    cols,
    sums_ref,
    bias_ref,
    out_ref,
    counts_ref,
    bias_out_ref,
    got_col,
    col_sum,
    got_row,
    send_sems,
    recv_sems,
):
    row, col = lax.axis_index("row"), lax.axis_index("col")
    greet((("row", rows), ("col", cols)))
    width = out_ref.shape[-1] // 3
    copies = [
        push(sums_ref.at[peer], got_col.at[step - 1], send_sems, recv_sems, step - 1, "col", peer)
        for step, peer in peers_of("col", cols)
    ]
    base = 2 * (cols - 1) + rows - 1
    bias_copies = [
        push(
            bias_ref.at[peer],
            bias_out_ref.at[col],
            send_sems,
            recv_sems,
            base + step - 1,
            "col",
            peer,
        )
        for step, peer in peers_of("col", cols)
    ]
    bias_out_ref[col] = bias_ref[col]
    total = sums_ref[col].astype(jnp.float32)
    for at, copy in enumerate(copies):
        copy.wait()
        total = total + got_col[at].astype(jnp.float32)
    col_sum[...] = total.reshape(col_sum.shape)
    base = cols - 1
    copies = [
        push(
            col_sum.at[peer],
            got_row.at[step - 1],
            send_sems,
            recv_sems,
            base + step - 1,
            "row",
            peer,
        )
        for step, peer in peers_of("row", rows)
    ]
    total = col_sum[row]
    for at, copy in enumerate(copies):
        copy.wait()
        total = total + got_row[at]
    counts = total[:, 2 * width :]
    counts_ref[...] = counts
    out_ref[col] = jnp.concatenate(
        [total[:, :width] / counts, total[:, width:]], axis=1
    ).astype(out_ref.dtype)
    base += rows - 1
    copies = [
        push(
            out_ref.at[col], out_ref.at[col], send_sems, recv_sems, base + step - 1, "col", peer
        )
        for step, peer in peers_of("col", cols)
    ]
    for copy in copies + bias_copies:
        copy.wait()


def pool_call(partial_sums, bias, share):
    rows, cols = lax.axis_size("row"), lax.axis_size("col")
    width = partial_sums.shape[-1]
    copies = 3 * (cols - 1) + rows - 1
    bias = bias.reshape((cols, -1) + bias.shape[1:])
    return pl.pallas_call(
        functools.partial(pool_kernel, rows, cols),
        out_shape=(
            jax.ShapeDtypeStruct((cols, share, width), jnp.bfloat16),
            jax.ShapeDtypeStruct((share, width // 3), jnp.float32),
            jax.ShapeDtypeStruct(bias.shape, bias.dtype),
        ),
        in_specs=[pl.BlockSpec(memory_space=pltpu.VMEM)] * 2,
        out_specs=(pl.BlockSpec(memory_space=pltpu.VMEM),) * 3,
        scratch_shapes=[
            pltpu.VMEM((cols - 1, rows * share, width), jnp.bfloat16),
            pltpu.VMEM((rows, share, width), jnp.float32),
            pltpu.VMEM((rows - 1, share, width), jnp.float32),
            pltpu.SemaphoreType.DMA((copies,)),
            pltpu.SemaphoreType.DMA((copies,)),
        ],
        compiler_params=pltpu.CompilerParams(collective_id=0, has_side_effects=True),
    )(partial_sums.reshape(cols, rows * share, width), bias)


def tail_kernel(
    rows,
    cols,
    both_ref,
    single_ref,
    grad_out_ref,
    normal_ref,
    inverse_ref,
    counts_ref,
    dec_ref,
    pool_ref,
    weight_ref,
    out_ref,
    weight_out_ref,
    got_both,
    held,
    row_weights,
    col_weights,
    send_sems,
    recv_sems,
):
    row, col = lax.axis_index("row"), lax.axis_index("col")
    greet((("row", rows), ("col", cols)))
    width = single_ref.shape[-1]
    copies = [
        push(both_ref.at[peer], got_both.at[step - 1], send_sems, recv_sems, step - 1, "col", peer)
        for step, peer in peers_of("col", cols)
    ]
    base = cols - 1
    row_weights[row] = weight_ref[...]
    weight_copies = [
        push(
            row_weights.at[row],
            row_weights.at[row],
            send_sems,
            recv_sems,
            base + step - 1,
            "row",
            peer,
        )
        for step, peer in peers_of("row", rows)
    ]
    base += rows - 1
    total = both_ref[col].astype(jnp.float32)
    for at, copy in enumerate(copies):
        copy.wait()
        total = total + got_both[at].astype(jnp.float32)
    token_out = (single_ref[...] + total[:, :width]).astype(jnp.bfloat16)
    token_back = jnp.dot(token_out, dec_ref[...], preferred_element_type=jnp.float32)
    grad_single = (
        grad_out_ref[...] + norm_grad(total[:, width:], normal_ref[...], inverse_ref[...])
    ).astype(jnp.bfloat16)
    token_grad = transposed_dot(grad_single, pool_ref[...]) / counts_ref[...]
    held[row] = jnp.concatenate([token_back, token_grad], axis=1).astype(jnp.bfloat16)
    copies = [
        push(held.at[row], held.at[row], send_sems, recv_sems, base + step - 1, "row", peer)
        for step, peer in peers_of("row", rows)
    ]
    base += rows - 1
    for copy in weight_copies:
        copy.wait()
    weight = row_weights[0]
    for at in range(1, rows):
        weight = weight + row_weights[at]
    col_weights[col] = weight
    weight_copies = [
        push(
            col_weights.at[col],
            col_weights.at[col],
            send_sems,
            recv_sems,
            base + step - 1,
            "col",
            peer,
        )
        for step, peer in peers_of("col", cols)
    ]
    base += cols - 1
    for copy in copies:
        copy.wait()
    copies = [
        push(held, out_ref.at[col], send_sems, recv_sems, base + step - 1, "col", peer)
        for step, peer in peers_of("col", cols)
    ]
    out_ref[col] = held[...]
    for copy in weight_copies:
        copy.wait()
    weight = col_weights[0]
    for at in range(1, cols):
        weight = weight + col_weights[at]
    weight_out_ref[...] = weight
    for copy in copies:
        copy.wait()


def tail_call(both, single, grad_out, normal, inverse, counts, w_dec, w_pool, weight):
    rows, cols = lax.axis_size("row"), lax.axis_size("col")
    share, atom_width = counts.shape
    copies = 3 * (cols - 1) + 2 * (rows - 1)
    return pl.pallas_call(
        functools.partial(tail_kernel, rows, cols),
        out_shape=(
            jax.ShapeDtypeStruct((cols, rows, share, 2 * atom_width), jnp.bfloat16),
            jax.ShapeDtypeStruct(weight.shape, jnp.float32),
        ),
        in_specs=[pl.BlockSpec(memory_space=pltpu.VMEM)] * 9,
        out_specs=(pl.BlockSpec(memory_space=pltpu.VMEM),) * 2,
        scratch_shapes=[
            pltpu.VMEM((cols - 1, share, both.shape[-1]), jnp.bfloat16),
            pltpu.VMEM((rows, share, 2 * atom_width), jnp.bfloat16),
            pltpu.VMEM((rows,) + weight.shape, jnp.float32),
            pltpu.VMEM((cols,) + weight.shape, jnp.float32),
            pltpu.SemaphoreType.DMA((copies,)),
            pltpu.SemaphoreType.DMA((copies,)),
        ],
        compiler_params=pltpu.CompilerParams(collective_id=1, has_side_effects=True),
    )(
        both.reshape(cols, share, -1),
        single,
        grad_out,
        normal,
        inverse,
        counts,
        w_dec,
        w_pool,
        weight,
    )


def on_device(
    atom_single, atom_token, atom_cot, token_cond, pair, w_pool, w_qkv, w_bias, w_out, w_dec
):
    tok_rows = token_cond.shape[0]
    total_tokens = tok_rows * lax.axis_size("row")
    width = w_out.shape[0]
    local_heads = width // HD
    atom_width = atom_single.shape[1]
    scale = 1.0 / math.sqrt(HD)
    share = tok_rows // lax.axis_size("col")
    onehot = (
        share_order(atom_token, tok_rows, share)[:, None]
        == jnp.arange(total_tokens, dtype=jnp.int32)[None, :]
    ).astype(jnp.bfloat16)
    stacked = jnp.concatenate([atom_single, atom_cot, jnp.ones_like(atom_cot)], axis=1)
    partial_sums = lax.dot_general(
        onehot, stacked, (((0,), (0,)), ((), ())), preferred_element_type=jnp.float32
    ).astype(jnp.bfloat16)
    bias_local = jnp.einsum("ijc,ch->hij", pair, w_bias, preferred_element_type=jnp.float32).astype(
        jnp.bfloat16
    )
    row_pooled, share_counts, bias_blocks = pool_call(partial_sums, bias_local, share)
    row_pooled = row_pooled.reshape(tok_rows, 3 * atom_width)
    pooled = row_pooled[:, :atom_width]
    cot_pooled = row_pooled[:, atom_width : 2 * atom_width]
    single = token_cond.astype(jnp.float32) + jnp.dot(
        pooled, w_pool, preferred_element_type=jnp.float32
    )
    normal, inverse = layer_norm(single)
    normed = normal.astype(jnp.bfloat16)
    projected = jnp.einsum("td,kdf->ktf", normed, w_qkv, preferred_element_type=jnp.float32).astype(
        jnp.bfloat16
    )
    gathered = jnp.swapaxes(gather(projected[1:], "row"), 0, 1)
    queries = projected[0].reshape(tok_rows, local_heads, HD)
    keys_all = gathered[0].reshape(total_tokens, local_heads, HD)
    values_all = gathered[1].reshape(total_tokens, local_heads, HD)
    bias_rows = jnp.transpose(bias_blocks, (1, 2, 0, 3)).reshape(
        local_heads, tok_rows, total_tokens
    )
    logits = jnp.einsum(
        "ihd,jhd->hij", queries, keys_all, preferred_element_type=jnp.float32
    ) * scale + bias_rows.astype(jnp.float32)
    shifted = jnp.exp(logits - jnp.max(logits, axis=-1, keepdims=True))
    probs = shifted / jnp.sum(shifted, axis=-1, keepdims=True)
    probs_low = probs.astype(jnp.bfloat16)
    attended = (
        jnp.einsum("hij,jhd->ihd", probs_low, values_all, preferred_element_type=jnp.float32)
        .astype(jnp.bfloat16)
        .reshape(tok_rows, width)
    )
    partial_update = jnp.dot(attended, w_out, preferred_element_type=jnp.float32)
    grad_out = transposed_dot(cot_pooled, w_dec)
    grad_update = grad_out.astype(jnp.bfloat16)
    grad_attended = (
        transposed_dot(grad_update, w_out).astype(jnp.bfloat16).reshape(tok_rows, local_heads, HD)
    )
    grad_probs = jnp.einsum(
        "ihd,jhd->hij", grad_attended, values_all, preferred_element_type=jnp.float32
    )
    delta = jnp.sum(probs * grad_probs, axis=-1, keepdims=True)
    grad_logits = (probs * (grad_probs - delta)).astype(jnp.bfloat16)
    grad_queries = (
        (
            jnp.einsum("hij,jhd->ihd", grad_logits, keys_all, preferred_element_type=jnp.float32)
            * scale
        )
        .astype(jnp.bfloat16)
        .reshape(tok_rows, width)
    )
    key_terms = jnp.stack(
        [
            jnp.einsum("hij,ihd->jhd", grad_logits, queries, preferred_element_type=jnp.float32),
            jnp.einsum(
                "hij,ihd->jhd", probs_low, grad_attended, preferred_element_type=jnp.float32
            ),
        ]
    ).reshape(2, total_tokens, width)
    key_blocks = jnp.swapaxes(
        key_terms.astype(jnp.bfloat16).reshape(2, -1, tok_rows, width), 0, 1
    )
    key_sums = jnp.sum(exchange_blocks(key_blocks, "row").astype(jnp.float32), axis=0)
    grad_keys = (key_sums[0] * scale).astype(jnp.bfloat16)
    grad_values = key_sums[1].astype(jnp.bfloat16)
    grad_proj = jnp.stack([grad_queries, grad_keys, grad_values])
    normed_part = jnp.einsum("ktf,kdf->td", grad_proj, w_qkv, preferred_element_type=jnp.float32)
    both = jnp.concatenate([partial_update, normed_part], axis=1).astype(jnp.bfloat16)
    bias_back = lax.all_to_all(grad_logits, "col", split_axis=2, concat_axis=0, tiled=True)
    weight_part = jnp.einsum("ijc,hij->hc", pair, bias_back, preferred_element_type=jnp.float32)

    def mine(rows):
        return lax.dynamic_slice_in_dim(rows, lax.axis_index("col") * share, share, axis=0)

    all_back, grad_bias = tail_call(
        both,
        mine(single),
        mine(grad_out),
        mine(normal),
        mine(inverse),
        share_counts,
        w_dec,
        w_pool,
        weight_part,
    )
    all_back = all_back.reshape(total_tokens, 2 * atom_width)
    grad_bias = grad_bias.T
    picked = jnp.dot(onehot, all_back, preferred_element_type=jnp.float32)
    atom_out = (atom_single.astype(jnp.float32) + picked[:, :atom_width]).astype(jnp.bfloat16)
    grad_atom = atom_cot.astype(jnp.float32) + picked[:, atom_width:]
    return (atom_out, grad_atom, grad_bias)


def solution(mesh):
    return jax.shard_map(
        on_device,
        mesh=mesh,
        in_specs=(
            P(("row", "col"), None),
            P(("row", "col")),
            P(("row", "col"), None),
            P("row", None),
            P("row", "col", None),
            P(),
            P(None, None, "col"),
            P(),
            P("col", None),
            P(),
        ),
        out_specs=(P(("row", "col"), None), P(("row", "col"), None), P()),
        check_vma=False,
    )
```

```python
import functools
import math

import jax
import jax.numpy as jnp
from jax import lax
from jax.experimental import pallas as pl
from jax.experimental.pallas import tpu as pltpu
from jax.sharding import PartitionSpec as P

HD = 48


EPSILON = 1e-05


def layer_norm(single):
    center = single - jnp.mean(single, axis=-1, keepdims=True)
    inverse = lax.rsqrt(jnp.mean(center * center, axis=-1, keepdims=True) + EPSILON)
    return (center * inverse, inverse)


def norm_grad(upstream, normal, inverse):
    return inverse * (
        upstream
        - jnp.mean(upstream, axis=-1, keepdims=True)
        - normal * jnp.mean(upstream * normal, axis=-1, keepdims=True)
    )


def transposed_dot(left, right):
    return lax.dot_general(
        left, right, (((1,), (1,)), ((), ())), preferred_element_type=jnp.float32
    )


def exchange_blocks(blocks, axis):
    return lax.all_to_all(blocks, axis, split_axis=0, concat_axis=0, tiled=True)


def gather(block, axis):
    return exchange_blocks(
        jnp.broadcast_to(block[None], (lax.axis_size(axis),) + block.shape), axis
    )


def share_order(token, tok_rows, share):
    row, inside = token // tok_rows, token % tok_rows
    return (inside // share * lax.axis_size("row") + row) * share + inside % share


def push(source, target, send_sems, recv_sems, at, axis, peer):
    copy = pltpu.make_async_remote_copy(
        src_ref=source,
        dst_ref=target,
        send_sem=send_sems.at[at],
        recv_sem=recv_sems.at[at],
        device_id={axis: peer},
        device_id_type=pl.DeviceIdType.MESH,
    )
    copy.start()
    return copy


def peers_of(axis, size):
    me = lax.axis_index(axis)
    return [(step, lax.rem(me + step, size)) for step in range(1, size)]


def greet(sizes):
    barrier = pltpu.get_barrier_semaphore()
    for axis, size in sizes:
        for _, peer in peers_of(axis, size):
            pl.semaphore_signal(
                barrier, inc=1, device_id={axis: peer}, device_id_type=pl.DeviceIdType.MESH
            )
    pl.semaphore_wait(barrier, sum(size - 1 for _, size in sizes))


def pool_kernel(
    rows,
    cols,
    sums_ref,
    bias_ref,
    out_ref,
    counts_ref,
    bias_out_ref,
    got_col,
    col_sum,
    got_row,
    send_sems,
    recv_sems,
):
    row, col = lax.axis_index("row"), lax.axis_index("col")
    greet((("row", rows), ("col", cols)))
    width = out_ref.shape[-1] // 3
    copies = [
        push(sums_ref.at[peer], got_col.at[step - 1], send_sems, recv_sems, step - 1, "col", peer)
        for step, peer in peers_of("col", cols)
    ]
    base = 2 * (cols - 1) + rows - 1
    bias_copies = [
        push(
            bias_ref.at[peer],
            bias_out_ref.at[col],
            send_sems,
            recv_sems,
            base + step - 1,
            "col",
            peer,
        )
        for step, peer in peers_of("col", cols)
    ]
    bias_out_ref[col] = bias_ref[col]
    total = sums_ref[col].astype(jnp.float32)
    for at, copy in enumerate(copies):
        copy.wait()
        total = total + got_col[at].astype(jnp.float32)
    col_sum[...] = total.reshape(col_sum.shape)
    base = cols - 1
    copies = [
        push(
            col_sum.at[peer],
            got_row.at[step - 1],
            send_sems,
            recv_sems,
            base + step - 1,
            "row",
            peer,
        )
        for step, peer in peers_of("row", rows)
    ]
    total = col_sum[row]
    for at, copy in enumerate(copies):
        copy.wait()
        total = total + got_row[at]
    counts = total[:, 2 * width :]
    counts_ref[...] = counts
    out_ref[col] = jnp.concatenate(
        [total[:, :width] / counts, total[:, width:]], axis=1
    ).astype(out_ref.dtype)
    base += rows - 1
    copies = [
        push(
            out_ref.at[col], out_ref.at[col], send_sems, recv_sems, base + step - 1, "col", peer
        )
        for step, peer in peers_of("col", cols)
    ]
    for copy in copies + bias_copies:
        copy.wait()


def pool_call(partial_sums, bias, share):
    rows, cols = lax.axis_size("row"), lax.axis_size("col")
    width = partial_sums.shape[-1]
    copies = 3 * (cols - 1) + rows - 1
    bias = bias.reshape((cols, -1) + bias.shape[1:])
    return pl.pallas_call(
        functools.partial(pool_kernel, rows, cols),
        out_shape=(
            jax.ShapeDtypeStruct((cols, share, width), jnp.bfloat16),
            jax.ShapeDtypeStruct((share, width // 3), jnp.float32),
            jax.ShapeDtypeStruct(bias.shape, bias.dtype),
        ),
        in_specs=[pl.BlockSpec(memory_space=pltpu.VMEM)] * 2,
        out_specs=(pl.BlockSpec(memory_space=pltpu.VMEM),) * 3,
        scratch_shapes=[
            pltpu.VMEM((cols - 1, rows * share, width), jnp.bfloat16),
            pltpu.VMEM((rows, share, width), jnp.float32),
            pltpu.VMEM((rows - 1, share, width), jnp.float32),
            pltpu.SemaphoreType.DMA((copies,)),
            pltpu.SemaphoreType.DMA((copies,)),
        ],
        compiler_params=pltpu.CompilerParams(collective_id=0, has_side_effects=True),
    )(partial_sums.reshape(cols, rows * share, width), bias)


def tail_kernel(
    rows,
    cols,
    both_ref,
    single_ref,
    grad_out_ref,
    normal_ref,
    inverse_ref,
    counts_ref,
    dec_ref,
    pool_ref,
    weight_ref,
    out_ref,
    weight_out_ref,
    got_both,
    held,
    row_weights,
    col_weights,
    send_sems,
    recv_sems,
):
    row, col = lax.axis_index("row"), lax.axis_index("col")
    greet((("row", rows), ("col", cols)))
    width = single_ref.shape[-1]
    copies = [
        push(both_ref.at[peer], got_both.at[step - 1], send_sems, recv_sems, step - 1, "col", peer)
        for step, peer in peers_of("col", cols)
    ]
    base = cols - 1
    row_weights[row] = weight_ref[...]
    weight_copies = [
        push(
            row_weights.at[row],
            row_weights.at[row],
            send_sems,
            recv_sems,
            base + step - 1,
            "row",
            peer,
        )
        for step, peer in peers_of("row", rows)
    ]
    base += rows - 1
    total = both_ref[col].astype(jnp.float32)
    for at, copy in enumerate(copies):
        copy.wait()
        total = total + got_both[at].astype(jnp.float32)
    token_out = (single_ref[...] + total[:, :width]).astype(jnp.bfloat16)
    token_back = jnp.dot(token_out, dec_ref[...], preferred_element_type=jnp.float32)
    grad_single = (
        grad_out_ref[...] + norm_grad(total[:, width:], normal_ref[...], inverse_ref[...])
    ).astype(jnp.bfloat16)
    token_grad = transposed_dot(grad_single, pool_ref[...]) / counts_ref[...]
    held[row] = jnp.concatenate([token_back, token_grad], axis=1).astype(jnp.bfloat16)
    copies = [
        push(held.at[row], held.at[row], send_sems, recv_sems, base + step - 1, "row", peer)
        for step, peer in peers_of("row", rows)
    ]
    base += rows - 1
    for copy in weight_copies:
        copy.wait()
    weight = row_weights[0]
    for at in range(1, rows):
        weight = weight + row_weights[at]
    col_weights[col] = weight
    weight_copies = [
        push(
            col_weights.at[col],
            col_weights.at[col],
            send_sems,
            recv_sems,
            base + step - 1,
            "col",
            peer,
        )
        for step, peer in peers_of("col", cols)
    ]
    base += cols - 1
    for copy in copies:
        copy.wait()
    copies = [
        push(held, out_ref.at[col], send_sems, recv_sems, base + step - 1, "col", peer)
        for step, peer in peers_of("col", cols)
    ]
    out_ref[col] = held[...]
    for copy in weight_copies:
        copy.wait()
    weight = col_weights[0]
    for at in range(1, cols):
        weight = weight + col_weights[at]
    weight_out_ref[...] = weight
    for copy in copies:
        copy.wait()


def tail_call(both, single, grad_out, normal, inverse, counts, w_dec, w_pool, weight):
    rows, cols = lax.axis_size("row"), lax.axis_size("col")
    share, atom_width = counts.shape
    copies = 3 * (cols - 1) + 2 * (rows - 1)
    return pl.pallas_call(
        functools.partial(tail_kernel, rows, cols),
        out_shape=(
            jax.ShapeDtypeStruct((cols, rows, share, 2 * atom_width), jnp.bfloat16),
            jax.ShapeDtypeStruct(weight.shape, jnp.float32),
        ),
        in_specs=[pl.BlockSpec(memory_space=pltpu.VMEM)] * 9,
        out_specs=(pl.BlockSpec(memory_space=pltpu.VMEM),) * 2,
        scratch_shapes=[
            pltpu.VMEM((cols - 1, share, both.shape[-1]), jnp.bfloat16),
            pltpu.VMEM((rows, share, 2 * atom_width), jnp.bfloat16),
            pltpu.VMEM((rows,) + weight.shape, jnp.float32),
            pltpu.VMEM((cols,) + weight.shape, jnp.float32),
            pltpu.SemaphoreType.DMA((copies,)),
            pltpu.SemaphoreType.DMA((copies,)),
        ],
        compiler_params=pltpu.CompilerParams(collective_id=1, has_side_effects=True),
    )(
        both.reshape(cols, share, -1),
        single,
        grad_out,
        normal,
        inverse,
        counts,
        w_dec,
        w_pool,
        weight,
    )


def on_device(
    atom_single, atom_token, atom_cot, token_cond, pair, w_pool, w_qkv, w_bias, w_out, w_dec
):
    tok_rows = token_cond.shape[0]
    total_tokens = tok_rows * lax.axis_size("row")
    width = w_out.shape[0]
    local_heads = width // HD
    atom_width = atom_single.shape[1]
    scale = 1.0 / math.sqrt(HD)
    share = tok_rows // lax.axis_size("col")
    onehot = (
        share_order(atom_token, tok_rows, share)[:, None]
        == jnp.arange(total_tokens, dtype=jnp.int32)[None, :]
    ).astype(jnp.bfloat16)
    stacked = jnp.concatenate([atom_single, atom_cot, jnp.ones_like(atom_cot)], axis=1)
    partial_sums = lax.dot_general(
        onehot, stacked, (((0,), (0,)), ((), ())), preferred_element_type=jnp.float32
    ).astype(jnp.bfloat16)
    bias_local = jnp.einsum("ijc,ch->hij", pair, w_bias, preferred_element_type=jnp.float32).astype(
        jnp.bfloat16
    )
    row_pooled, share_counts, bias_blocks = pool_call(partial_sums, bias_local, share)
    row_pooled = row_pooled.reshape(tok_rows, 3 * atom_width)
    pooled = row_pooled[:, :atom_width]
    cot_pooled = row_pooled[:, atom_width : 2 * atom_width]
    single = token_cond.astype(jnp.float32) + jnp.dot(
        pooled, w_pool, preferred_element_type=jnp.float32
    )
    normal, inverse = layer_norm(single)
    normed = normal.astype(jnp.bfloat16)
    projected = jnp.einsum("td,kdf->ktf", normed, w_qkv, preferred_element_type=jnp.float32).astype(
        jnp.bfloat16
    )
    gathered = jnp.swapaxes(gather(projected[1:], "row"), 0, 1)
    queries = projected[0].reshape(tok_rows, local_heads, HD)
    keys_all = gathered[0].reshape(total_tokens, local_heads, HD)
    values_all = gathered[1].reshape(total_tokens, local_heads, HD)
    bias_rows = jnp.transpose(bias_blocks, (1, 2, 0, 3)).reshape(
        local_heads, tok_rows, total_tokens
    )
    logits = jnp.einsum(
        "ihd,jhd->hij", queries, keys_all, preferred_element_type=jnp.float32
    ) * scale + bias_rows.astype(jnp.float32)
    shifted = jnp.exp(logits - jnp.max(logits, axis=-1, keepdims=True))
    probs = shifted / jnp.sum(shifted, axis=-1, keepdims=True)
    probs_low = probs.astype(jnp.bfloat16)
    attended = (
        jnp.einsum("hij,jhd->ihd", probs_low, values_all, preferred_element_type=jnp.float32)
        .astype(jnp.bfloat16)
        .reshape(tok_rows, width)
    )
    partial_update = jnp.dot(attended, w_out, preferred_element_type=jnp.float32)
    grad_out = transposed_dot(cot_pooled, w_dec)
    grad_update = grad_out.astype(jnp.bfloat16)
    grad_attended = (
        transposed_dot(grad_update, w_out).astype(jnp.bfloat16).reshape(tok_rows, local_heads, HD)
    )
    grad_probs = jnp.einsum(
        "ihd,jhd->hij", grad_attended, values_all, preferred_element_type=jnp.float32
    )
    delta = jnp.sum(probs * grad_probs, axis=-1, keepdims=True)
    grad_logits = (probs * (grad_probs - delta)).astype(jnp.bfloat16)
    grad_queries = (
        (
            jnp.einsum("hij,jhd->ihd", grad_logits, keys_all, preferred_element_type=jnp.float32)
            * scale
        )
        .astype(jnp.bfloat16)
        .reshape(tok_rows, width)
    )
    key_terms = jnp.stack(
        [
            jnp.einsum("hij,ihd->jhd", grad_logits, queries, preferred_element_type=jnp.float32),
            jnp.einsum(
                "hij,ihd->jhd", probs_low, grad_attended, preferred_element_type=jnp.float32
            ),
        ]
    ).reshape(2, total_tokens, width)
    key_blocks = jnp.swapaxes(
        key_terms.astype(jnp.bfloat16).reshape(2, -1, tok_rows, width), 0, 1
    )
    bias_back = lax.all_to_all(grad_logits, "col", split_axis=2, concat_axis=0, tiled=True)
    key_blocks, bias_back = lax.optimization_barrier((key_blocks, bias_back))
    key_sums = jnp.sum(exchange_blocks(key_blocks, "row").astype(jnp.float32), axis=0)
    grad_keys = (key_sums[0] * scale).astype(jnp.bfloat16)
    grad_values = key_sums[1].astype(jnp.bfloat16)
    grad_proj = jnp.stack([grad_queries, grad_keys, grad_values])
    normed_part = jnp.einsum("ktf,kdf->td", grad_proj, w_qkv, preferred_element_type=jnp.float32)
    both = jnp.concatenate([partial_update, normed_part], axis=1).astype(jnp.bfloat16)
    weight_part = jnp.einsum("ijc,hij->hc", pair, bias_back, preferred_element_type=jnp.float32)

    def mine(rows):
        return lax.dynamic_slice_in_dim(rows, lax.axis_index("col") * share, share, axis=0)

    all_back, grad_bias = tail_call(
        both,
        mine(single),
        mine(grad_out),
        mine(normal),
        mine(inverse),
        share_counts,
        w_dec,
        w_pool,
        weight_part,
    )
    all_back = all_back.reshape(total_tokens, 2 * atom_width)
    grad_bias = grad_bias.T
    picked = jnp.dot(onehot, all_back, preferred_element_type=jnp.float32)
    atom_out = (atom_single.astype(jnp.float32) + picked[:, :atom_width]).astype(jnp.bfloat16)
    grad_atom = atom_cot.astype(jnp.float32) + picked[:, atom_width:]
    return (atom_out, grad_atom, grad_bias)


def solution(mesh):
    return jax.shard_map(
        on_device,
        mesh=mesh,
        in_specs=(
            P(("row", "col"), None),
            P(("row", "col")),
            P(("row", "col"), None),
            P("row", None),
            P("row", "col", None),
            P(),
            P(None, None, "col"),
            P(),
            P("col", None),
            P(),
        ),
        out_specs=(P(("row", "col"), None), P(("row", "col"), None), P()),
        check_vma=False,
    )
```

```python
import functools
import math

import jax
import jax.numpy as jnp
from jax import lax
from jax.experimental import pallas as pl
from jax.experimental.pallas import tpu as pltpu
from jax.sharding import PartitionSpec as P

HD = 48


EPSILON = 1e-05


def layer_norm(single):
    center = single - jnp.mean(single, axis=-1, keepdims=True)
    inverse = lax.rsqrt(jnp.mean(center * center, axis=-1, keepdims=True) + EPSILON)
    return (center * inverse, inverse)


def norm_grad(upstream, normal, inverse):
    return inverse * (
        upstream
        - jnp.mean(upstream, axis=-1, keepdims=True)
        - normal * jnp.mean(upstream * normal, axis=-1, keepdims=True)
    )


def transposed_dot(left, right):
    return lax.dot_general(
        left, right, (((1,), (1,)), ((), ())), preferred_element_type=jnp.float32
    )


def exchange_blocks(blocks, axis):
    return lax.all_to_all(blocks, axis, split_axis=0, concat_axis=0, tiled=True)


def gather(block, axis):
    return exchange_blocks(
        jnp.broadcast_to(block[None], (lax.axis_size(axis),) + block.shape), axis
    )


def share_order(token, tok_rows, share):
    row, inside = token // tok_rows, token % tok_rows
    return (inside // share * lax.axis_size("row") + row) * share + inside % share


def push(source, target, send_sems, recv_sems, at, axis, peer):
    copy = pltpu.make_async_remote_copy(
        src_ref=source,
        dst_ref=target,
        send_sem=send_sems.at[at],
        recv_sem=recv_sems.at[at],
        device_id={axis: peer},
        device_id_type=pl.DeviceIdType.MESH,
    )
    copy.start()
    return copy


def peers_of(axis, size):
    me = lax.axis_index(axis)
    return [(step, lax.rem(me + step, size)) for step in range(1, size)]


def greet(sizes):
    barrier = pltpu.get_barrier_semaphore()
    for axis, size in sizes:
        for _, peer in peers_of(axis, size):
            pl.semaphore_signal(
                barrier, inc=1, device_id={axis: peer}, device_id_type=pl.DeviceIdType.MESH
            )
    pl.semaphore_wait(barrier, sum(size - 1 for _, size in sizes))


def pool_kernel(
    rows,
    cols,
    sums_ref,
    tally_ref,
    bias_ref,
    out_ref,
    counts_ref,
    bias_out_ref,
    got_row,
    row_sum,
    got_col,
    row_tally,
    sum_tally,
    col_tally,
    all_tally,
    send_sems,
    recv_sems,
):
    row, col = lax.axis_index("row"), lax.axis_index("col")
    greet((("row", rows), ("col", cols)))
    share, width = out_ref.shape[1:]
    base = 0

    def send_all(axis, size, source, target):
        nonlocal base
        copies = [
            push(
                source(peer), target(step - 1), send_sems, recv_sems, base + step - 1, axis, peer
            )
            for step, peer in peers_of(axis, size)
        ]
        base += size - 1
        return copies

    sums = send_all("row", rows, lambda peer: sums_ref.at[:, peer], lambda at: got_row.at[at])
    tallies = send_all("row", rows, lambda peer: tally_ref.at[peer], lambda at: row_tally.at[at])
    bias_copies = send_all(
        "col", cols, lambda peer: bias_ref.at[peer], lambda at: bias_out_ref.at[col]
    )
    bias_out_ref[col] = bias_ref[col]
    tally = tally_ref[row]
    for at, copy in enumerate(tallies):
        copy.wait()
        tally = tally + row_tally[at]
    sum_tally[...] = tally
    tallies = send_all("col", cols, lambda peer: sum_tally, lambda at: col_tally.at[at])
    total = sums_ref[:, row].astype(jnp.float32)
    for at, copy in enumerate(sums):
        copy.wait()
        total = total + got_row[at].astype(jnp.float32)
    row_sum[...] = total
    sums = send_all("col", cols, lambda peer: row_sum.at[peer], lambda at: got_col.at[at])
    for at, copy in enumerate(tallies):
        copy.wait()
        tally = tally + col_tally[at]
    all_tally[...] = tally
    mine = jnp.broadcast_to(all_tally[pl.ds(col, 1), :], (share, tally.shape[1]))
    diagonal = lax.broadcasted_iota(jnp.int32, mine.shape, 0) == lax.broadcasted_iota(
        jnp.int32, mine.shape, 1
    )
    counts = jnp.sum(jnp.where(diagonal, mine, 0.0), axis=1, keepdims=True)
    counts_ref[...] = jnp.broadcast_to(counts, counts_ref.shape)
    total = row_sum[col]
    for at, copy in enumerate(sums):
        copy.wait()
        total = total + got_col[at]
    half = width // 2
    out_ref[col] = jnp.concatenate([total[:, :half] / counts, total[:, half:]], axis=1).astype(
        out_ref.dtype
    )
    copies = send_all("col", cols, lambda peer: out_ref.at[col], lambda at: out_ref.at[col])
    for copy in copies + bias_copies:
        copy.wait()


def pool_call(partial_sums, partial_counts, bias, share):
    rows, cols = lax.axis_size("row"), lax.axis_size("col")
    width = partial_sums.shape[-1]
    copies = 4 * (cols - 1) + 2 * (rows - 1)
    bias = bias.reshape((cols, -1) + bias.shape[1:])
    lanes = width // 2
    tally = jnp.swapaxes(partial_counts.reshape(cols, rows, share), 0, 1)
    tally = jnp.pad(tally, ((0, 0), (0, 0), (0, lanes - share)))
    return pl.pallas_call(
        functools.partial(pool_kernel, rows, cols),
        out_shape=(
            jax.ShapeDtypeStruct((cols, share, width), jnp.bfloat16),
            jax.ShapeDtypeStruct((share, width // 2), jnp.float32),
            jax.ShapeDtypeStruct(bias.shape, bias.dtype),
        ),
        in_specs=[pl.BlockSpec(memory_space=pltpu.VMEM)] * 3,
        out_specs=(pl.BlockSpec(memory_space=pltpu.VMEM),) * 3,
        scratch_shapes=[
            pltpu.VMEM((rows - 1, cols, share, width), jnp.bfloat16),
            pltpu.VMEM((cols, share, width), jnp.float32),
            pltpu.VMEM((cols - 1, share, width), jnp.float32),
            pltpu.VMEM((rows - 1, cols, lanes), jnp.float32),
            pltpu.VMEM((cols, lanes), jnp.float32),
            pltpu.VMEM((cols - 1, cols, lanes), jnp.float32),
            pltpu.VMEM((cols, lanes), jnp.float32),
            pltpu.SemaphoreType.DMA((copies,)),
            pltpu.SemaphoreType.DMA((copies,)),
        ],
        compiler_params=pltpu.CompilerParams(collective_id=0, has_side_effects=True),
    )(partial_sums.reshape(cols, rows, share, width), tally, bias)


def tail_kernel(
    rows,
    cols,
    both_ref,
    single_ref,
    grad_out_ref,
    normal_ref,
    inverse_ref,
    counts_ref,
    dec_ref,
    pool_ref,
    weight_ref,
    out_ref,
    weight_out_ref,
    got_both,
    held,
    row_weights,
    col_weights,
    send_sems,
    recv_sems,
):
    row, col = lax.axis_index("row"), lax.axis_index("col")
    greet((("row", rows), ("col", cols)))
    width = single_ref.shape[-1]
    copies = [
        push(both_ref.at[peer], got_both.at[step - 1], send_sems, recv_sems, step - 1, "col", peer)
        for step, peer in peers_of("col", cols)
    ]
    base = cols - 1
    row_weights[row] = weight_ref[...]
    weight_copies = [
        push(
            row_weights.at[row],
            row_weights.at[row],
            send_sems,
            recv_sems,
            base + step - 1,
            "row",
            peer,
        )
        for step, peer in peers_of("row", rows)
    ]
    base += rows - 1
    total = both_ref[col].astype(jnp.float32)
    for at, copy in enumerate(copies):
        copy.wait()
        total = total + got_both[at].astype(jnp.float32)
    token_out = (single_ref[...] + total[:, :width]).astype(jnp.bfloat16)
    token_back = jnp.dot(token_out, dec_ref[...], preferred_element_type=jnp.float32)
    grad_single = (
        grad_out_ref[...] + norm_grad(total[:, width:], normal_ref[...], inverse_ref[...])
    ).astype(jnp.bfloat16)
    token_grad = transposed_dot(grad_single, pool_ref[...]) / counts_ref[...]
    held[row] = jnp.concatenate([token_back, token_grad], axis=1).astype(jnp.bfloat16)
    copies = [
        push(held.at[row], held.at[row], send_sems, recv_sems, base + step - 1, "row", peer)
        for step, peer in peers_of("row", rows)
    ]
    base += rows - 1
    for copy in weight_copies:
        copy.wait()
    weight = row_weights[0]
    for at in range(1, rows):
        weight = weight + row_weights[at]
    col_weights[col] = weight
    weight_copies = [
        push(
            col_weights.at[col],
            col_weights.at[col],
            send_sems,
            recv_sems,
            base + step - 1,
            "col",
            peer,
        )
        for step, peer in peers_of("col", cols)
    ]
    base += cols - 1
    for copy in copies:
        copy.wait()
    copies = [
        push(held, out_ref.at[col], send_sems, recv_sems, base + step - 1, "col", peer)
        for step, peer in peers_of("col", cols)
    ]
    out_ref[col] = held[...]
    for copy in weight_copies:
        copy.wait()
    weight = col_weights[0]
    for at in range(1, cols):
        weight = weight + col_weights[at]
    weight_out_ref[...] = weight
    for copy in copies:
        copy.wait()


def tail_call(both, single, grad_out, normal, inverse, counts, w_dec, w_pool, weight):
    rows, cols = lax.axis_size("row"), lax.axis_size("col")
    share, atom_width = counts.shape
    copies = 3 * (cols - 1) + 2 * (rows - 1)
    return pl.pallas_call(
        functools.partial(tail_kernel, rows, cols),
        out_shape=(
            jax.ShapeDtypeStruct((cols, rows, share, 2 * atom_width), jnp.bfloat16),
            jax.ShapeDtypeStruct(weight.shape, jnp.float32),
        ),
        in_specs=[pl.BlockSpec(memory_space=pltpu.VMEM)] * 9,
        out_specs=(pl.BlockSpec(memory_space=pltpu.VMEM),) * 2,
        scratch_shapes=[
            pltpu.VMEM((cols - 1, share, both.shape[-1]), jnp.bfloat16),
            pltpu.VMEM((rows, share, 2 * atom_width), jnp.bfloat16),
            pltpu.VMEM((rows,) + weight.shape, jnp.float32),
            pltpu.VMEM((cols,) + weight.shape, jnp.float32),
            pltpu.SemaphoreType.DMA((copies,)),
            pltpu.SemaphoreType.DMA((copies,)),
        ],
        compiler_params=pltpu.CompilerParams(collective_id=1, has_side_effects=True),
    )(
        both.reshape(cols, share, -1),
        single,
        grad_out,
        normal,
        inverse,
        counts,
        w_dec,
        w_pool,
        weight,
    )


def on_device(
    atom_single, atom_token, atom_cot, token_cond, pair, w_pool, w_qkv, w_bias, w_out, w_dec
):
    tok_rows = token_cond.shape[0]
    total_tokens = tok_rows * lax.axis_size("row")
    width = w_out.shape[0]
    local_heads = width // HD
    atom_width = atom_single.shape[1]
    scale = 1.0 / math.sqrt(HD)
    share = tok_rows // lax.axis_size("col")
    onehot = (
        share_order(atom_token, tok_rows, share)[:, None]
        == jnp.arange(total_tokens, dtype=jnp.int32)[None, :]
    ).astype(jnp.bfloat16)
    stacked = jnp.concatenate([atom_single, atom_cot], axis=1)
    partial_sums = lax.dot_general(
        onehot, stacked, (((0,), (0,)), ((), ())), preferred_element_type=jnp.float32
    ).astype(jnp.bfloat16)
    partial_counts = jnp.sum(onehot.astype(jnp.float32), axis=0)
    bias_local = jnp.einsum("ijc,ch->hij", pair, w_bias, preferred_element_type=jnp.float32).astype(
        jnp.bfloat16
    )
    row_pooled, share_counts, bias_blocks = pool_call(
        partial_sums, partial_counts, bias_local, share
    )
    row_pooled = row_pooled.reshape(tok_rows, 2 * atom_width)
    pooled = row_pooled[:, :atom_width]
    cot_pooled = row_pooled[:, atom_width : 2 * atom_width]
    single = token_cond.astype(jnp.float32) + jnp.dot(
        pooled, w_pool, preferred_element_type=jnp.float32
    )
    normal, inverse = layer_norm(single)
    normed = normal.astype(jnp.bfloat16)
    projected = jnp.einsum("td,kdf->ktf", normed, w_qkv, preferred_element_type=jnp.float32).astype(
        jnp.bfloat16
    )
    gathered = jnp.swapaxes(gather(projected[1:], "row"), 0, 1)
    queries = projected[0].reshape(tok_rows, local_heads, HD)
    keys_all = gathered[0].reshape(total_tokens, local_heads, HD)
    values_all = gathered[1].reshape(total_tokens, local_heads, HD)
    bias_rows = jnp.transpose(bias_blocks, (1, 2, 0, 3)).reshape(
        local_heads, tok_rows, total_tokens
    )
    logits = jnp.einsum(
        "ihd,jhd->hij", queries, keys_all, preferred_element_type=jnp.float32
    ) * scale + bias_rows.astype(jnp.float32)
    shifted = jnp.exp(logits - jnp.max(logits, axis=-1, keepdims=True))
    probs = shifted / jnp.sum(shifted, axis=-1, keepdims=True)
    probs_low = probs.astype(jnp.bfloat16)
    attended = (
        jnp.einsum("hij,jhd->ihd", probs_low, values_all, preferred_element_type=jnp.float32)
        .astype(jnp.bfloat16)
        .reshape(tok_rows, width)
    )
    partial_update = jnp.dot(attended, w_out, preferred_element_type=jnp.float32)
    grad_out = transposed_dot(cot_pooled, w_dec)
    grad_update = grad_out.astype(jnp.bfloat16)
    grad_attended = (
        transposed_dot(grad_update, w_out).astype(jnp.bfloat16).reshape(tok_rows, local_heads, HD)
    )
    grad_probs = jnp.einsum(
        "ihd,jhd->hij", grad_attended, values_all, preferred_element_type=jnp.float32
    )
    delta = jnp.sum(probs * grad_probs, axis=-1, keepdims=True)
    grad_logits = (probs * (grad_probs - delta)).astype(jnp.bfloat16)
    grad_queries = (
        (
            jnp.einsum("hij,jhd->ihd", grad_logits, keys_all, preferred_element_type=jnp.float32)
            * scale
        )
        .astype(jnp.bfloat16)
        .reshape(tok_rows, width)
    )
    key_terms = jnp.stack(
        [
            jnp.einsum("hij,ihd->jhd", grad_logits, queries, preferred_element_type=jnp.float32),
            jnp.einsum(
                "hij,ihd->jhd", probs_low, grad_attended, preferred_element_type=jnp.float32
            ),
        ]
    ).reshape(2, total_tokens, width)
    key_blocks = jnp.swapaxes(
        key_terms.astype(jnp.bfloat16).reshape(2, -1, tok_rows, width), 0, 1
    )
    bias_back = lax.all_to_all(grad_logits, "col", split_axis=2, concat_axis=0, tiled=True)
    key_blocks, bias_back = lax.optimization_barrier((key_blocks, bias_back))
    key_sums = jnp.sum(exchange_blocks(key_blocks, "row").astype(jnp.float32), axis=0)
    grad_keys = (key_sums[0] * scale).astype(jnp.bfloat16)
    grad_values = key_sums[1].astype(jnp.bfloat16)
    grad_proj = jnp.stack([grad_queries, grad_keys, grad_values])
    normed_part = jnp.einsum("ktf,kdf->td", grad_proj, w_qkv, preferred_element_type=jnp.float32)
    both = jnp.concatenate([partial_update, normed_part], axis=1).astype(jnp.bfloat16)
    weight_part = jnp.einsum("ijc,hij->hc", pair, bias_back, preferred_element_type=jnp.float32)

    def mine(rows):
        return lax.dynamic_slice_in_dim(rows, lax.axis_index("col") * share, share, axis=0)

    all_back, grad_bias = tail_call(
        both,
        mine(single),
        mine(grad_out),
        mine(normal),
        mine(inverse),
        share_counts,
        w_dec,
        w_pool,
        weight_part,
    )
    all_back = all_back.reshape(total_tokens, 2 * atom_width)
    grad_bias = grad_bias.T
    picked = jnp.dot(onehot, all_back, preferred_element_type=jnp.float32)
    atom_out = (atom_single.astype(jnp.float32) + picked[:, :atom_width]).astype(jnp.bfloat16)
    grad_atom = atom_cot.astype(jnp.float32) + picked[:, atom_width:]
    return (atom_out, grad_atom, grad_bias)


def solution(mesh):
    return jax.shard_map(
        on_device,
        mesh=mesh,
        in_specs=(
            P(("row", "col"), None),
            P(("row", "col")),
            P(("row", "col"), None),
            P("row", None),
            P("row", "col", None),
            P(),
            P(None, None, "col"),
            P(),
            P("col", None),
            P(),
        ),
        out_specs=(P(("row", "col"), None), P(("row", "col"), None), P()),
        check_vma=False,
    )
```

```python
import functools
import math

import jax
import jax.numpy as jnp
from jax import lax
from jax.experimental import pallas as pl
from jax.experimental.pallas import tpu as pltpu
from jax.sharding import PartitionSpec as P

HD = 48


EPSILON = 1e-05


def layer_norm(single):
    center = single - jnp.mean(single, axis=-1, keepdims=True)
    inverse = lax.rsqrt(jnp.mean(center * center, axis=-1, keepdims=True) + EPSILON)
    return (center * inverse, inverse)


def norm_grad(upstream, normal, inverse):
    return inverse * (
        upstream
        - jnp.mean(upstream, axis=-1, keepdims=True)
        - normal * jnp.mean(upstream * normal, axis=-1, keepdims=True)
    )


def transposed_dot(left, right):
    return lax.dot_general(
        left, right, (((1,), (1,)), ((), ())), preferred_element_type=jnp.float32
    )


def exchange_blocks(blocks, axis):
    return lax.all_to_all(blocks, axis, split_axis=0, concat_axis=0, tiled=True)


def gather(block, axis):
    return exchange_blocks(
        jnp.broadcast_to(block[None], (lax.axis_size(axis),) + block.shape), axis
    )


def share_order(token, tok_rows, share):
    row, inside = token // tok_rows, token % tok_rows
    return (inside // share * lax.axis_size("row") + row) * share + inside % share


def push(source, target, send_sems, recv_sems, at, axis, peer):
    copy = pltpu.make_async_remote_copy(
        src_ref=source,
        dst_ref=target,
        send_sem=send_sems.at[at],
        recv_sem=recv_sems.at[at],
        device_id={axis: peer},
        device_id_type=pl.DeviceIdType.MESH,
    )
    copy.start()
    return copy


def peers_of(axis, size):
    me = lax.axis_index(axis)
    return [(step, lax.rem(me + step, size)) for step in range(1, size)]


def greet(sizes):
    barrier = pltpu.get_barrier_semaphore()
    for axis, size in sizes:
        for _, peer in peers_of(axis, size):
            pl.semaphore_signal(
                barrier, inc=1, device_id={axis: peer}, device_id_type=pl.DeviceIdType.MESH
            )
    pl.semaphore_wait(barrier, sum(size - 1 for _, size in sizes))


def pool_kernel(
    rows,
    cols,
    sums_ref,
    tally_ref,
    bias_ref,
    out_ref,
    counts_ref,
    bias_out_ref,
    got_row,
    row_sum,
    got_col,
    row_tally,
    sum_tally,
    col_tally,
    all_tally,
    send_sems,
    recv_sems,
):
    row, col = lax.axis_index("row"), lax.axis_index("col")
    greet((("row", rows), ("col", cols)))
    share, width = out_ref.shape[1:]
    base = 0

    def send_all(axis, size, source, target):
        nonlocal base
        copies = [
            push(
                source(peer), target(step - 1), send_sems, recv_sems, base + step - 1, axis, peer
            )
            for step, peer in peers_of(axis, size)
        ]
        base += size - 1
        return copies

    sums = send_all("row", rows, lambda peer: sums_ref.at[:, peer], lambda at: got_row.at[at])
    tallies = send_all("row", rows, lambda peer: tally_ref.at[peer], lambda at: row_tally.at[at])
    bias_copies = send_all(
        "col", cols, lambda peer: bias_ref.at[peer], lambda at: bias_out_ref.at[col]
    )
    bias_out_ref[col] = bias_ref[col]
    tally = tally_ref[row]
    for at, copy in enumerate(tallies):
        copy.wait()
        tally = tally + row_tally[at]
    sum_tally[...] = tally
    tallies = send_all("col", cols, lambda peer: sum_tally, lambda at: col_tally.at[at])
    total = sums_ref[:, row].astype(jnp.float32)
    for at, copy in enumerate(sums):
        copy.wait()
        total = total + got_row[at].astype(jnp.float32)
    row_sum[...] = total
    sums = send_all("col", cols, lambda peer: row_sum.at[peer], lambda at: got_col.at[at])
    for at, copy in enumerate(tallies):
        copy.wait()
        tally = tally + col_tally[at]
    all_tally[...] = tally
    mine = jnp.broadcast_to(all_tally[pl.ds(col, 1), :], (share, tally.shape[1]))
    diagonal = lax.broadcasted_iota(jnp.int32, mine.shape, 0) == lax.broadcasted_iota(
        jnp.int32, mine.shape, 1
    )
    counts = jnp.sum(jnp.where(diagonal, mine, 0.0), axis=1, keepdims=True)
    counts_ref[...] = jnp.broadcast_to(counts, counts_ref.shape)
    total = row_sum[col]
    for at, copy in enumerate(sums):
        copy.wait()
        total = total + got_col[at]
    half = width // 2
    out_ref[col] = jnp.concatenate([total[:, :half] / counts, total[:, half:]], axis=1).astype(
        out_ref.dtype
    )
    copies = send_all("col", cols, lambda peer: out_ref.at[col], lambda at: out_ref.at[col])
    for copy in copies + bias_copies:
        copy.wait()


def pool_call(partial_sums, partial_counts, bias, share):
    rows, cols = lax.axis_size("row"), lax.axis_size("col")
    width = partial_sums.shape[-1]
    copies = 4 * (cols - 1) + 2 * (rows - 1)
    bias = bias.reshape((cols, -1) + bias.shape[1:])
    lanes = width // 2
    tally = jnp.swapaxes(partial_counts.reshape(cols, rows, share), 0, 1)
    tally = jnp.pad(tally, ((0, 0), (0, 0), (0, lanes - share)))
    return pl.pallas_call(
        functools.partial(pool_kernel, rows, cols),
        out_shape=(
            jax.ShapeDtypeStruct((cols, share, width), jnp.bfloat16),
            jax.ShapeDtypeStruct((share, width // 2), jnp.float32),
            jax.ShapeDtypeStruct(bias.shape, bias.dtype),
        ),
        in_specs=[pl.BlockSpec(memory_space=pltpu.VMEM)] * 3,
        out_specs=(pl.BlockSpec(memory_space=pltpu.VMEM),) * 3,
        scratch_shapes=[
            pltpu.VMEM((rows - 1, cols, share, width), jnp.bfloat16),
            pltpu.VMEM((cols, share, width), jnp.float32),
            pltpu.VMEM((cols - 1, share, width), jnp.float32),
            pltpu.VMEM((rows - 1, cols, lanes), jnp.float32),
            pltpu.VMEM((cols, lanes), jnp.float32),
            pltpu.VMEM((cols - 1, cols, lanes), jnp.float32),
            pltpu.VMEM((cols, lanes), jnp.float32),
            pltpu.SemaphoreType.DMA((copies,)),
            pltpu.SemaphoreType.DMA((copies,)),
        ],
        compiler_params=pltpu.CompilerParams(collective_id=0, has_side_effects=True),
    )(partial_sums.reshape(cols, rows, share, width), tally, bias)


def tail_kernel(
    rows,
    cols,
    both_ref,
    single_ref,
    grad_out_ref,
    normal_ref,
    inverse_ref,
    counts_ref,
    dec_ref,
    pool_ref,
    weight_ref,
    out_ref,
    weight_out_ref,
    got_pair,
    pair_sum,
    got_both,
    held,
    row_weights,
    col_weights,
    send_sems,
    recv_sems,
):
    row, col = lax.axis_index("row"), lax.axis_index("col")
    greet((("row", rows), ("col", cols)))
    width = single_ref.shape[-1]
    chips = cols // 2
    chip, side = col // 2, lax.rem(col, 2)
    other = 1 - side
    partner = chip * 2 + other
    order = [(step, lax.rem(chip + step, chips)) for step in range(1, chips)] + [(0, chip)]
    pair_copies = [
        push(
            both_ref.at[target, other],
            got_pair.at[step],
            send_sems,
            recv_sems,
            step,
            "col",
            partner,
        )
        for step, target in order
    ]
    base = 2 * chips - 1
    row_weights[row] = weight_ref[...]
    weight_copies = [
        push(
            row_weights.at[row],
            row_weights.at[row],
            send_sems,
            recv_sems,
            base + step - 1,
            "row",
            peer,
        )
        for step, peer in peers_of("row", rows)
    ]
    base += rows - 1
    copies = []
    for (step, target), pair_copy in zip(order, pair_copies):
        pair_copy.wait()
        total = both_ref[target, side].astype(jnp.float32) + got_pair[step].astype(jnp.float32)
        if step > 0:
            pair_sum[step - 1] = total.astype(jnp.bfloat16)
            copies.append(
                push(
                    pair_sum.at[step - 1],
                    got_both.at[step - 1],
                    send_sems,
                    recv_sems,
                    chips + step - 1,
                    "col",
                    target * 2 + side,
                )
            )
    for at, copy in enumerate(copies):
        copy.wait()
        total = total + got_both[at].astype(jnp.float32)
    token_out = (single_ref[...] + total[:, :width]).astype(jnp.bfloat16)
    token_back = jnp.dot(token_out, dec_ref[...], preferred_element_type=jnp.float32)
    grad_single = (
        grad_out_ref[...] + norm_grad(total[:, width:], normal_ref[...], inverse_ref[...])
    ).astype(jnp.bfloat16)
    token_grad = transposed_dot(grad_single, pool_ref[...]) / counts_ref[...]
    held[row] = jnp.concatenate([token_back, token_grad], axis=1).astype(jnp.bfloat16)
    copies = [
        push(held.at[row], held.at[row], send_sems, recv_sems, base + step - 1, "row", peer)
        for step, peer in peers_of("row", rows)
    ]
    base += rows - 1
    for copy in weight_copies:
        copy.wait()
    weight = row_weights[0]
    for at in range(1, rows):
        weight = weight + row_weights[at]
    col_weights[col] = weight
    weight_copies = [
        push(
            col_weights.at[col],
            col_weights.at[col],
            send_sems,
            recv_sems,
            base + step - 1,
            "col",
            peer,
        )
        for step, peer in peers_of("col", cols)
    ]
    base += cols - 1
    for copy in copies:
        copy.wait()
    far_copies = [
        push(
            held,
            out_ref.at[col],
            send_sems,
            recv_sems,
            base + step - 1,
            "col",
            target * 2 + side,
        )
        for step, target in order
        if step > 0
    ]
    base += chips - 1
    copies = [push(held, out_ref.at[col], send_sems, recv_sems, base, "col", partner)]
    out_ref[col] = held[...]
    for copy in weight_copies:
        copy.wait()
    weight = col_weights[0]
    for at in range(1, cols):
        weight = weight + col_weights[at]
    weight_out_ref[...] = weight
    for step, copy in enumerate(far_copies, 1):
        copy.wait()
        source = lax.rem(chip - step + chips, chips) * 2 + side
        copies.append(
            push(
                out_ref.at[source],
                out_ref.at[source],
                send_sems,
                recv_sems,
                base + step,
                "col",
                partner,
            )
        )
    for copy in copies:
        copy.wait()


def tail_call(both, single, grad_out, normal, inverse, counts, w_dec, w_pool, weight):
    rows, cols = lax.axis_size("row"), lax.axis_size("col")
    share, atom_width = counts.shape
    chips = cols // 2
    copies = 2 * (2 * chips - 1) + cols - 1 + 2 * (rows - 1)
    return pl.pallas_call(
        functools.partial(tail_kernel, rows, cols),
        out_shape=(
            jax.ShapeDtypeStruct((cols, rows, share, 2 * atom_width), jnp.bfloat16),
            jax.ShapeDtypeStruct(weight.shape, jnp.float32),
        ),
        in_specs=[pl.BlockSpec(memory_space=pltpu.VMEM)] * 9,
        out_specs=(pl.BlockSpec(memory_space=pltpu.VMEM),) * 2,
        scratch_shapes=[
            pltpu.VMEM((chips, share, both.shape[-1]), jnp.bfloat16),
            pltpu.VMEM((chips - 1, share, both.shape[-1]), jnp.bfloat16),
            pltpu.VMEM((chips - 1, share, both.shape[-1]), jnp.bfloat16),
            pltpu.VMEM((rows, share, 2 * atom_width), jnp.bfloat16),
            pltpu.VMEM((rows,) + weight.shape, jnp.float32),
            pltpu.VMEM((cols,) + weight.shape, jnp.float32),
            pltpu.SemaphoreType.DMA((copies,)),
            pltpu.SemaphoreType.DMA((copies,)),
        ],
        compiler_params=pltpu.CompilerParams(collective_id=1, has_side_effects=True),
    )(
        both.reshape(chips, 2, share, -1),
        single,
        grad_out,
        normal,
        inverse,
        counts,
        w_dec,
        w_pool,
        weight,
    )


def on_device(
    atom_single, atom_token, atom_cot, token_cond, pair, w_pool, w_qkv, w_bias, w_out, w_dec
):
    tok_rows = token_cond.shape[0]
    total_tokens = tok_rows * lax.axis_size("row")
    width = w_out.shape[0]
    local_heads = width // HD
    atom_width = atom_single.shape[1]
    scale = 1.0 / math.sqrt(HD)
    share = tok_rows // lax.axis_size("col")
    onehot = (
        share_order(atom_token, tok_rows, share)[:, None]
        == jnp.arange(total_tokens, dtype=jnp.int32)[None, :]
    ).astype(jnp.bfloat16)
    stacked = jnp.concatenate([atom_single, atom_cot], axis=1)
    partial_sums = lax.dot_general(
        onehot, stacked, (((0,), (0,)), ((), ())), preferred_element_type=jnp.float32
    ).astype(jnp.bfloat16)
    partial_counts = jnp.sum(onehot.astype(jnp.float32), axis=0)
    bias_local = jnp.einsum("ijc,ch->hij", pair, w_bias, preferred_element_type=jnp.float32).astype(
        jnp.bfloat16
    )
    row_pooled, share_counts, bias_blocks = pool_call(
        partial_sums, partial_counts, bias_local, share
    )
    row_pooled = row_pooled.reshape(tok_rows, 2 * atom_width)
    pooled = row_pooled[:, :atom_width]
    cot_pooled = row_pooled[:, atom_width : 2 * atom_width]
    single = token_cond.astype(jnp.float32) + jnp.dot(
        pooled, w_pool, preferred_element_type=jnp.float32
    )
    normal, inverse = layer_norm(single)
    normed = normal.astype(jnp.bfloat16)
    projected = jnp.einsum("td,kdf->ktf", normed, w_qkv, preferred_element_type=jnp.float32).astype(
        jnp.bfloat16
    )
    gathered = jnp.swapaxes(gather(projected[1:], "row"), 0, 1)
    queries = projected[0].reshape(tok_rows, local_heads, HD)
    keys_all = gathered[0].reshape(total_tokens, local_heads, HD)
    values_all = gathered[1].reshape(total_tokens, local_heads, HD)
    bias_rows = jnp.transpose(bias_blocks, (1, 2, 0, 3)).reshape(
        local_heads, tok_rows, total_tokens
    )
    logits = jnp.einsum(
        "ihd,jhd->hij", queries, keys_all, preferred_element_type=jnp.float32
    ) * scale + bias_rows.astype(jnp.float32)
    shifted = jnp.exp(logits - jnp.max(logits, axis=-1, keepdims=True))
    probs = shifted / jnp.sum(shifted, axis=-1, keepdims=True)
    probs_low = probs.astype(jnp.bfloat16)
    attended = (
        jnp.einsum("hij,jhd->ihd", probs_low, values_all, preferred_element_type=jnp.float32)
        .astype(jnp.bfloat16)
        .reshape(tok_rows, width)
    )
    partial_update = jnp.dot(attended, w_out, preferred_element_type=jnp.float32)
    grad_out = transposed_dot(cot_pooled, w_dec)
    grad_update = grad_out.astype(jnp.bfloat16)
    grad_attended = (
        transposed_dot(grad_update, w_out).astype(jnp.bfloat16).reshape(tok_rows, local_heads, HD)
    )
    grad_probs = jnp.einsum(
        "ihd,jhd->hij", grad_attended, values_all, preferred_element_type=jnp.float32
    )
    delta = jnp.sum(probs * grad_probs, axis=-1, keepdims=True)
    grad_logits = (probs * (grad_probs - delta)).astype(jnp.bfloat16)
    grad_queries = (
        (
            jnp.einsum("hij,jhd->ihd", grad_logits, keys_all, preferred_element_type=jnp.float32)
            * scale
        )
        .astype(jnp.bfloat16)
        .reshape(tok_rows, width)
    )
    key_terms = jnp.stack(
        [
            jnp.einsum("hij,ihd->jhd", grad_logits, queries, preferred_element_type=jnp.float32),
            jnp.einsum(
                "hij,ihd->jhd", probs_low, grad_attended, preferred_element_type=jnp.float32
            ),
        ]
    ).reshape(2, total_tokens, width)
    key_blocks = jnp.swapaxes(
        key_terms.astype(jnp.bfloat16).reshape(2, -1, tok_rows, width), 0, 1
    )
    bias_back = lax.all_to_all(grad_logits, "col", split_axis=2, concat_axis=0, tiled=True)
    key_blocks, bias_back = lax.optimization_barrier((key_blocks, bias_back))
    key_sums = jnp.sum(exchange_blocks(key_blocks, "row").astype(jnp.float32), axis=0)
    grad_keys = (key_sums[0] * scale).astype(jnp.bfloat16)
    grad_values = key_sums[1].astype(jnp.bfloat16)
    grad_proj = jnp.stack([grad_queries, grad_keys, grad_values])
    normed_part = jnp.einsum("ktf,kdf->td", grad_proj, w_qkv, preferred_element_type=jnp.float32)
    both = jnp.concatenate([partial_update, normed_part], axis=1).astype(jnp.bfloat16)
    weight_part = jnp.einsum("ijc,hij->hc", pair, bias_back, preferred_element_type=jnp.float32)

    def mine(rows):
        return lax.dynamic_slice_in_dim(rows, lax.axis_index("col") * share, share, axis=0)

    all_back, grad_bias = tail_call(
        both,
        mine(single),
        mine(grad_out),
        mine(normal),
        mine(inverse),
        share_counts,
        w_dec,
        w_pool,
        weight_part,
    )
    all_back = all_back.reshape(total_tokens, 2 * atom_width)
    grad_bias = grad_bias.T
    picked = jnp.dot(onehot, all_back, preferred_element_type=jnp.float32)
    atom_out = (atom_single.astype(jnp.float32) + picked[:, :atom_width]).astype(jnp.bfloat16)
    grad_atom = atom_cot.astype(jnp.float32) + picked[:, atom_width:]
    return (atom_out, grad_atom, grad_bias)


def solution(mesh):
    return jax.shard_map(
        on_device,
        mesh=mesh,
        in_specs=(
            P(("row", "col"), None),
            P(("row", "col")),
            P(("row", "col"), None),
            P("row", None),
            P("row", "col", None),
            P(),
            P(None, None, "col"),
            P(),
            P("col", None),
            P(),
        ),
        out_specs=(P(("row", "col"), None), P(("row", "col"), None), P()),
        check_vma=False,
    )
```

```python
import functools
import math

import jax
import jax.numpy as jnp
from jax import lax
from jax.experimental import pallas as pl
from jax.experimental.pallas import tpu as pltpu
from jax.sharding import PartitionSpec as P

HD = 48


EPSILON = 1e-05


def layer_norm(single):
    center = single - jnp.mean(single, axis=-1, keepdims=True)
    inverse = lax.rsqrt(jnp.mean(center * center, axis=-1, keepdims=True) + EPSILON)
    return (center * inverse, inverse)


def norm_grad(upstream, normal, inverse):
    return inverse * (
        upstream
        - jnp.mean(upstream, axis=-1, keepdims=True)
        - normal * jnp.mean(upstream * normal, axis=-1, keepdims=True)
    )


def transposed_dot(left, right):
    return lax.dot_general(
        left, right, (((1,), (1,)), ((), ())), preferred_element_type=jnp.float32
    )


def exchange_blocks(blocks, axis):
    return lax.all_to_all(blocks, axis, split_axis=0, concat_axis=0, tiled=True)


def gather(block, axis):
    return exchange_blocks(
        jnp.broadcast_to(block[None], (lax.axis_size(axis),) + block.shape), axis
    )


def share_order(token, tok_rows, share):
    row, inside = token // tok_rows, token % tok_rows
    return (inside // share * lax.axis_size("row") + row) * share + inside % share


def push(source, target, send_sems, recv_sems, at, axis, peer):
    copy = pltpu.make_async_remote_copy(
        src_ref=source,
        dst_ref=target,
        send_sem=send_sems.at[at],
        recv_sem=recv_sems.at[at],
        device_id={axis: peer},
        device_id_type=pl.DeviceIdType.MESH,
    )
    copy.start()
    return copy


def peers_of(axis, size):
    me = lax.axis_index(axis)
    if size & (size - 1) == 0:
        return [(step, me ^ step) for step in range(1, size)]
    return [(step, lax.rem(me + step, size)) for step in range(1, size)]


def greet(sizes):
    barrier = pltpu.get_barrier_semaphore()
    for axis, size in sizes:
        for _, peer in peers_of(axis, size):
            pl.semaphore_signal(
                barrier, inc=1, device_id={axis: peer}, device_id_type=pl.DeviceIdType.MESH
            )
    pl.semaphore_wait(barrier, sum(size - 1 for _, size in sizes))


def pool_kernel(
    rows,
    cols,
    sums_ref,
    tally_ref,
    bias_ref,
    out_ref,
    counts_ref,
    bias_out_ref,
    got_row,
    row_sum,
    got_col,
    row_tally,
    sum_tally,
    col_tally,
    all_tally,
    send_sems,
    recv_sems,
):
    row, col = lax.axis_index("row"), lax.axis_index("col")
    greet((("row", rows), ("col", cols)))
    share, width = out_ref.shape[1:]
    base = 0

    def send_all(axis, size, source, target):
        nonlocal base
        copies = [
            push(
                source(peer), target(step - 1), send_sems, recv_sems, base + step - 1, axis, peer
            )
            for step, peer in peers_of(axis, size)
        ]
        base += size - 1
        return copies

    sums = send_all("row", rows, lambda peer: sums_ref.at[:, peer], lambda at: got_row.at[at])
    tallies = send_all("row", rows, lambda peer: tally_ref.at[peer], lambda at: row_tally.at[at])
    bias_copies = send_all(
        "col", cols, lambda peer: bias_ref.at[peer], lambda at: bias_out_ref.at[col]
    )
    bias_out_ref[col] = bias_ref[col]
    tally = tally_ref[row]
    for at, copy in enumerate(tallies):
        copy.wait()
        tally = tally + row_tally[at]
    sum_tally[...] = tally
    tallies = send_all("col", cols, lambda peer: sum_tally, lambda at: col_tally.at[at])
    total = sums_ref[:, row].astype(jnp.float32)
    for at, copy in enumerate(sums):
        copy.wait()
        total = total + got_row[at].astype(jnp.float32)
    row_sum[...] = total
    sums = send_all("col", cols, lambda peer: row_sum.at[peer], lambda at: got_col.at[at])
    for at, copy in enumerate(tallies):
        copy.wait()
        tally = tally + col_tally[at]
    all_tally[...] = tally
    mine = jnp.broadcast_to(all_tally[pl.ds(col, 1), :], (share, tally.shape[1]))
    diagonal = lax.broadcasted_iota(jnp.int32, mine.shape, 0) == lax.broadcasted_iota(
        jnp.int32, mine.shape, 1
    )
    counts = jnp.sum(jnp.where(diagonal, mine, 0.0), axis=1, keepdims=True)
    counts_ref[...] = jnp.broadcast_to(counts, counts_ref.shape)
    total = row_sum[col]
    for at, copy in enumerate(sums):
        copy.wait()
        total = total + got_col[at]
    half = width // 2
    out_ref[col] = jnp.concatenate([total[:, :half] / counts, total[:, half:]], axis=1).astype(
        out_ref.dtype
    )
    copies = send_all("col", cols, lambda peer: out_ref.at[col], lambda at: out_ref.at[col])
    for copy in copies + bias_copies:
        copy.wait()


def pool_call(partial_sums, partial_counts, bias, share):
    rows, cols = lax.axis_size("row"), lax.axis_size("col")
    width = partial_sums.shape[-1]
    copies = 4 * (cols - 1) + 2 * (rows - 1)
    bias = bias.reshape((cols, -1) + bias.shape[1:])
    lanes = width // 2
    tally = jnp.swapaxes(partial_counts.reshape(cols, rows, share), 0, 1)
    tally = jnp.pad(tally, ((0, 0), (0, 0), (0, lanes - share)))
    return pl.pallas_call(
        functools.partial(pool_kernel, rows, cols),
        out_shape=(
            jax.ShapeDtypeStruct((cols, share, width), jnp.bfloat16),
            jax.ShapeDtypeStruct((share, width // 2), jnp.float32),
            jax.ShapeDtypeStruct(bias.shape, bias.dtype),
        ),
        in_specs=[pl.BlockSpec(memory_space=pltpu.VMEM)] * 3,
        out_specs=(pl.BlockSpec(memory_space=pltpu.VMEM),) * 3,
        scratch_shapes=[
            pltpu.VMEM((rows - 1, cols, share, width), jnp.bfloat16),
            pltpu.VMEM((cols, share, width), jnp.float32),
            pltpu.VMEM((cols - 1, share, width), jnp.float32),
            pltpu.VMEM((rows - 1, cols, lanes), jnp.float32),
            pltpu.VMEM((cols, lanes), jnp.float32),
            pltpu.VMEM((cols - 1, cols, lanes), jnp.float32),
            pltpu.VMEM((cols, lanes), jnp.float32),
            pltpu.SemaphoreType.DMA((copies,)),
            pltpu.SemaphoreType.DMA((copies,)),
        ],
        compiler_params=pltpu.CompilerParams(collective_id=0, has_side_effects=True),
    )(partial_sums.reshape(cols, rows, share, width), tally, bias)


def tail_kernel(
    rows,
    cols,
    both_ref,
    single_ref,
    grad_out_ref,
    normal_ref,
    inverse_ref,
    counts_ref,
    dec_ref,
    pool_ref,
    weight_ref,
    out_ref,
    weight_out_ref,
    got_pair,
    pair_sum,
    got_both,
    held,
    row_weights,
    col_weights,
    send_sems,
    recv_sems,
):
    row, col = lax.axis_index("row"), lax.axis_index("col")
    greet((("row", rows), ("col", cols)))
    width = single_ref.shape[-1]
    chips = cols // 2
    chip, side = col // 2, lax.rem(col, 2)
    other = 1 - side
    partner = chip * 2 + other
    order = [(step, lax.rem(chip + step, chips)) for step in range(1, chips)] + [(0, chip)]
    pair_copies = [
        push(
            both_ref.at[target, other],
            got_pair.at[step],
            send_sems,
            recv_sems,
            step,
            "col",
            partner,
        )
        for step, target in order
    ]
    base = 2 * chips - 1
    row_weights[row] = weight_ref[...]
    weight_copies = [
        push(
            row_weights.at[row],
            row_weights.at[row],
            send_sems,
            recv_sems,
            base + step - 1,
            "row",
            peer,
        )
        for step, peer in peers_of("row", rows)
    ]
    base += rows - 1
    copies = []
    for (step, target), pair_copy in zip(order, pair_copies):
        pair_copy.wait()
        total = both_ref[target, side].astype(jnp.float32) + got_pair[step].astype(jnp.float32)
        if step > 0:
            pair_sum[step - 1] = total.astype(jnp.bfloat16)
            copies.append(
                push(
                    pair_sum.at[step - 1],
                    got_both.at[step - 1],
                    send_sems,
                    recv_sems,
                    chips + step - 1,
                    "col",
                    target * 2 + side,
                )
            )
    for at, copy in enumerate(copies):
        copy.wait()
        total = total + got_both[at].astype(jnp.float32)
    token_out = (single_ref[...] + total[:, :width]).astype(jnp.bfloat16)
    token_back = jnp.dot(token_out, dec_ref[...], preferred_element_type=jnp.float32)
    grad_single = (
        grad_out_ref[...] + norm_grad(total[:, width:], normal_ref[...], inverse_ref[...])
    ).astype(jnp.bfloat16)
    token_grad = transposed_dot(grad_single, pool_ref[...]) / counts_ref[...]
    held[row] = jnp.concatenate([token_back, token_grad], axis=1).astype(jnp.bfloat16)
    copies = [
        push(held.at[row], held.at[row], send_sems, recv_sems, base + step - 1, "row", peer)
        for step, peer in peers_of("row", rows)
    ]
    base += rows - 1
    for copy in weight_copies:
        copy.wait()
    weight = row_weights[0]
    for at in range(1, rows):
        weight = weight + row_weights[at]
    col_weights[col] = weight
    weight_copies = [
        push(
            col_weights.at[col],
            col_weights.at[col],
            send_sems,
            recv_sems,
            base + step - 1,
            "col",
            peer,
        )
        for step, peer in peers_of("col", cols)
    ]
    base += cols - 1
    for copy in copies:
        copy.wait()
    far_copies = [
        push(
            held,
            out_ref.at[col],
            send_sems,
            recv_sems,
            base + step - 1,
            "col",
            target * 2 + side,
        )
        for step, target in order
        if step > 0
    ]
    base += chips - 1
    copies = [push(held, out_ref.at[col], send_sems, recv_sems, base, "col", partner)]
    out_ref[col] = held[...]
    for copy in weight_copies:
        copy.wait()
    weight = col_weights[0]
    for at in range(1, cols):
        weight = weight + col_weights[at]
    weight_out_ref[...] = weight
    for step, copy in enumerate(far_copies, 1):
        copy.wait()
        source = lax.rem(chip - step + chips, chips) * 2 + side
        copies.append(
            push(
                out_ref.at[source],
                out_ref.at[source],
                send_sems,
                recv_sems,
                base + step,
                "col",
                partner,
            )
        )
    for copy in copies:
        copy.wait()


def tail_call(both, single, grad_out, normal, inverse, counts, w_dec, w_pool, weight):
    rows, cols = lax.axis_size("row"), lax.axis_size("col")
    share, atom_width = counts.shape
    chips = cols // 2
    copies = 2 * (2 * chips - 1) + cols - 1 + 2 * (rows - 1)
    return pl.pallas_call(
        functools.partial(tail_kernel, rows, cols),
        out_shape=(
            jax.ShapeDtypeStruct((cols, rows, share, 2 * atom_width), jnp.bfloat16),
            jax.ShapeDtypeStruct(weight.shape, jnp.float32),
        ),
        in_specs=[pl.BlockSpec(memory_space=pltpu.VMEM)] * 9,
        out_specs=(pl.BlockSpec(memory_space=pltpu.VMEM),) * 2,
        scratch_shapes=[
            pltpu.VMEM((chips, share, both.shape[-1]), jnp.bfloat16),
            pltpu.VMEM((chips - 1, share, both.shape[-1]), jnp.bfloat16),
            pltpu.VMEM((chips - 1, share, both.shape[-1]), jnp.bfloat16),
            pltpu.VMEM((rows, share, 2 * atom_width), jnp.bfloat16),
            pltpu.VMEM((rows,) + weight.shape, jnp.float32),
            pltpu.VMEM((cols,) + weight.shape, jnp.float32),
            pltpu.SemaphoreType.DMA((copies,)),
            pltpu.SemaphoreType.DMA((copies,)),
        ],
        compiler_params=pltpu.CompilerParams(collective_id=1, has_side_effects=True),
    )(
        both.reshape(chips, 2, share, -1),
        single,
        grad_out,
        normal,
        inverse,
        counts,
        w_dec,
        w_pool,
        weight,
    )


def on_device(
    atom_single, atom_token, atom_cot, token_cond, pair, w_pool, w_qkv, w_bias, w_out, w_dec
):
    tok_rows = token_cond.shape[0]
    total_tokens = tok_rows * lax.axis_size("row")
    width = w_out.shape[0]
    local_heads = width // HD
    atom_width = atom_single.shape[1]
    scale = 1.0 / math.sqrt(HD)
    share = tok_rows // lax.axis_size("col")
    onehot = (
        share_order(atom_token, tok_rows, share)[:, None]
        == jnp.arange(total_tokens, dtype=jnp.int32)[None, :]
    ).astype(jnp.bfloat16)
    stacked = jnp.concatenate([atom_single, atom_cot], axis=1)
    partial_sums = lax.dot_general(
        onehot, stacked, (((0,), (0,)), ((), ())), preferred_element_type=jnp.float32
    ).astype(jnp.bfloat16)
    partial_counts = jnp.sum(onehot.astype(jnp.float32), axis=0)
    bias_local = jnp.einsum("ijc,ch->hij", pair, w_bias, preferred_element_type=jnp.float32).astype(
        jnp.bfloat16
    )
    row_pooled, share_counts, bias_blocks = pool_call(
        partial_sums, partial_counts, bias_local, share
    )
    row_pooled = row_pooled.reshape(tok_rows, 2 * atom_width)
    pooled = row_pooled[:, :atom_width]
    cot_pooled = row_pooled[:, atom_width : 2 * atom_width]
    single = token_cond.astype(jnp.float32) + jnp.dot(
        pooled, w_pool, preferred_element_type=jnp.float32
    )
    normal, inverse = layer_norm(single)
    normed = normal.astype(jnp.bfloat16)
    projected = jnp.einsum("td,kdf->ktf", normed, w_qkv, preferred_element_type=jnp.float32).astype(
        jnp.bfloat16
    )
    gathered = jnp.swapaxes(gather(projected[1:], "row"), 0, 1)
    queries = projected[0].reshape(tok_rows, local_heads, HD)
    keys_all = gathered[0].reshape(total_tokens, local_heads, HD)
    values_all = gathered[1].reshape(total_tokens, local_heads, HD)
    bias_rows = jnp.transpose(bias_blocks, (1, 2, 0, 3)).reshape(
        local_heads, tok_rows, total_tokens
    )
    logits = jnp.einsum(
        "ihd,jhd->hij", queries, keys_all, preferred_element_type=jnp.float32
    ) * scale + bias_rows.astype(jnp.float32)
    shifted = jnp.exp(logits - jnp.max(logits, axis=-1, keepdims=True))
    probs = shifted / jnp.sum(shifted, axis=-1, keepdims=True)
    probs_low = probs.astype(jnp.bfloat16)
    attended = (
        jnp.einsum("hij,jhd->ihd", probs_low, values_all, preferred_element_type=jnp.float32)
        .astype(jnp.bfloat16)
        .reshape(tok_rows, width)
    )
    partial_update = jnp.dot(attended, w_out, preferred_element_type=jnp.float32)
    grad_out = transposed_dot(cot_pooled, w_dec)
    grad_update = grad_out.astype(jnp.bfloat16)
    grad_attended = (
        transposed_dot(grad_update, w_out).astype(jnp.bfloat16).reshape(tok_rows, local_heads, HD)
    )
    grad_probs = jnp.einsum(
        "ihd,jhd->hij", grad_attended, values_all, preferred_element_type=jnp.float32
    )
    delta = jnp.sum(probs * grad_probs, axis=-1, keepdims=True)
    grad_logits = (probs * (grad_probs - delta)).astype(jnp.bfloat16)
    grad_queries = (
        (
            jnp.einsum("hij,jhd->ihd", grad_logits, keys_all, preferred_element_type=jnp.float32)
            * scale
        )
        .astype(jnp.bfloat16)
        .reshape(tok_rows, width)
    )
    key_terms = jnp.stack(
        [
            jnp.einsum("hij,ihd->jhd", grad_logits, queries, preferred_element_type=jnp.float32),
            jnp.einsum(
                "hij,ihd->jhd", probs_low, grad_attended, preferred_element_type=jnp.float32
            ),
        ]
    ).reshape(2, total_tokens, width)
    key_blocks = jnp.swapaxes(
        key_terms.astype(jnp.bfloat16).reshape(2, -1, tok_rows, width), 0, 1
    )
    bias_back = lax.all_to_all(grad_logits, "col", split_axis=2, concat_axis=0, tiled=True)
    key_blocks, bias_back = lax.optimization_barrier((key_blocks, bias_back))
    key_sums = jnp.sum(exchange_blocks(key_blocks, "row").astype(jnp.float32), axis=0)
    grad_keys = (key_sums[0] * scale).astype(jnp.bfloat16)
    grad_values = key_sums[1].astype(jnp.bfloat16)
    grad_proj = jnp.stack([grad_queries, grad_keys, grad_values])
    normed_part = jnp.einsum("ktf,kdf->td", grad_proj, w_qkv, preferred_element_type=jnp.float32)
    both = jnp.concatenate([partial_update, normed_part], axis=1).astype(jnp.bfloat16)
    weight_part = jnp.einsum("ijc,hij->hc", pair, bias_back, preferred_element_type=jnp.float32)

    def mine(rows):
        return lax.dynamic_slice_in_dim(rows, lax.axis_index("col") * share, share, axis=0)

    all_back, grad_bias = tail_call(
        both,
        mine(single),
        mine(grad_out),
        mine(normal),
        mine(inverse),
        share_counts,
        w_dec,
        w_pool,
        weight_part,
    )
    all_back = all_back.reshape(total_tokens, 2 * atom_width)
    grad_bias = grad_bias.T
    picked = jnp.dot(onehot, all_back, preferred_element_type=jnp.float32)
    atom_out = (atom_single.astype(jnp.float32) + picked[:, :atom_width]).astype(jnp.bfloat16)
    grad_atom = atom_cot.astype(jnp.float32) + picked[:, atom_width:]
    return (atom_out, grad_atom, grad_bias)


def solution(mesh):
    return jax.shard_map(
        on_device,
        mesh=mesh,
        in_specs=(
            P(("row", "col"), None),
            P(("row", "col")),
            P(("row", "col"), None),
            P("row", None),
            P("row", "col", None),
            P(),
            P(None, None, "col"),
            P(),
            P("col", None),
            P(),
        ),
        out_specs=(P(("row", "col"), None), P(("row", "col"), None), P()),
        check_vma=False,
    )
```
